512 devices in a mesh: blk: 8 (over z), wide: 64 (over y, x, core).
Axes of the slice: x: 4, y: 8, z: 8, core: 2. Of those that a mesh axis runs over, the one named last changes fastest.
Arguments:
- resid: bfloat16 [8192, 4096], P('wide', 'blk'), may hold values from -24 to 24
- samples: bfloat16 [8192, 4096], P('wide', 'blk'), may hold values from -6 to 6
- precision: float32 [64, 8, 8, 128, 128], P('wide', 'blk'), as said below
- active: int32 [64, 8, 8], P('wide', 'blk'), may hold values 0 or 1
Outputs:
- updated: float32 [64, 8, 8, 128, 128], P('wide', 'blk')
The draws below stay inside these ranges and needn't reach their ends.
Inputs may be any that keep to these rules, and one draw needn't show every extreme that they name: `precision`: entries on the diagonal of W lie between 1 and 2.
All inputs are finite; a program needn't handle non-finite values. No bound on the sum of `active` on one device may be relied on, other than what follows from the above.
Results may differ from the reference program's by a relative error of at most 0.0003.
Values may be sent and summed in bfloat16 or wider, within the bound.
No kernel may reach another device: no remote copies, remote signals or barrier semaphores. Data moves between devices by JAX's collectives and lax.ppermute only.
A program may use at most 128 MiB of HBM per device.

```python
import jax
import jax.numpy as jnp
from jax import lax

P_SIZE = 8192
TILE = 128
N = 4096
TILES = 64
TPC = 8
N_BLK = 8


def draw_precision(key, part):
    first_key, second_key = jax.random.split(key, 2)
    full_shape = (TILES, N_BLK, TPC, TILE, TILE)
    off_part = 0.1 * jax.random.normal(first_key, full_shape, jnp.float32)
    diag_part = jax.random.uniform(second_key, full_shape, jnp.float32, 1.0, 2.0)
    row_tile = lax.broadcasted_iota(jnp.int32, full_shape, 0)
    class_index = lax.broadcasted_iota(jnp.int32, full_shape, 1)
    within_index = lax.broadcasted_iota(jnp.int32, full_shape, 2)
    inner_row = lax.broadcasted_iota(jnp.int32, full_shape, 3)
    inner_column = lax.broadcasted_iota(jnp.int32, full_shape, 4)
    column_tile = (class_index - row_tile) % N_BLK + N_BLK * within_index
    on_diag = (column_tile == row_tile) & (inner_row == inner_column)
    return jnp.where(on_diag, diag_part, off_part)


def place_ends(drawn, rng, low, top_value):
    place = [jax.random.randint(jax.random.fold_in(rng, axis), (), 0, length) for axis, length in enumerate(drawn.shape)]
    main_axis = drawn.shape.index(max(drawn.shape))
    neighbour = place[:main_axis] + [(place[main_axis] + 1) % drawn.shape[main_axis]] + place[main_axis + 1:]
    return drawn.at[tuple(place)].set(low).at[tuple(neighbour)].set(top_value)


def block_levels(stream_key, dims, shards, smallest, top_value):
    def one(dim, parts):
        steps = jax.random.uniform(jax.random.fold_in(jax.random.fold_in(stream_key, 6), dim), (parts,), jnp.float32, smallest / len(shards), top_value / len(shards))
        return jnp.repeat(jnp.exp(steps), dims[dim] // parts).reshape((-1,) + (1,) * (len(dims) - dim - 1))

    gain = one(*shards[0])
    for cut in shards[1:]:
        gain = gain * one(*cut)
    return gain


def scatter_about(own_key, dims, deviation, most, shards=(), kind=jnp.bfloat16):
    result = deviation * jax.random.normal(own_key, dims, jnp.float32)
    if shards:
        result = result * block_levels(own_key, dims, shards, -0.22, 0.18)
    return jnp.clip(result, -most, most).astype(kind)


def setup_inputs(seed: int = 0) -> dict:
    seeds = jax.random.split(jax.random.key(seed), 5)
    return {
        "resid": scatter_about(seeds[0], (P_SIZE, N), 4.0, 24.0, ((0, 64), (1, 8))),
        "samples": scatter_about(seeds[1], (P_SIZE, N), 1.0, 6.0, ((0, 64), (1, 8))),
        "precision": draw_precision(jax.random.fold_in(seeds[4], 71), 0),
        "active": place_ends((jax.random.randint(seeds[3], (TILES, N_BLK, TPC), 0, 4) < 3).astype(jnp.int32), jax.random.fold_in(seeds[3], 1), 0, 1),
    }


STEP = 1.0
LASSO = 0.1
RIDGE = 0.5


def class_columns(row_ids, groups, per_class):
    classes = jnp.arange(groups, dtype=jnp.int32)
    within = jnp.arange(per_class, dtype=jnp.int32)
    return (classes[None, :, None] - row_ids[:, None, None]) % groups + groups * within[None, None, :]


def reference(resid, samples, precision, active):
    total_samples = resid.shape[1]
    tiles = precision.shape[0]
    groups = precision.shape[1]
    per_class = precision.shape[2]
    tile_size = precision.shape[3]
    gram = jnp.dot(resid, samples.T, preferred_element_type=jnp.float32) / total_samples
    gram_tiles = gram.reshape(tiles, tile_size, tiles, tile_size).transpose(0, 2, 1, 3)
    row_ids = jnp.arange(tiles, dtype=jnp.int32)
    column_ids = class_columns(row_ids, groups, per_class)
    forward = gram_tiles[row_ids[:, None, None], column_ids]
    backward = jnp.swapaxes(gram_tiles[column_ids, row_ids[:, None, None]], 3, 4)
    symmetric = 0.5 * (forward + backward)
    same_tile = column_ids == row_ids[:, None, None]
    identity = jnp.eye(tile_size, dtype=bool)
    on_diag = same_tile[:, :, :, None, None] & identity
    inverse = jnp.where(on_diag, 1.0 / jnp.where(on_diag, precision, 1.0), 0.0)
    stepped = precision - STEP * (symmetric + RIDGE * precision - inverse)
    shrunk = jnp.sign(stepped) * jnp.maximum(jnp.abs(stepped) - STEP * LASSO, 0.0)
    active_flags = active.astype(precision.dtype)
    return jnp.where(on_diag, stepped, shrunk) * active_flags[:, :, :, None, None]
```

```python
import functools

import jax
import jax.numpy as jnp
from jax import lax
from jax.experimental import pallas as pl
from jax.experimental.pallas import tpu as pltpu
from jax.sharding import Mesh, PartitionSpec as P

STEP = 1.0
LASSO = 0.1
RIDGE = 0.5
AXES = ("z", "y", "k")


def products(n, half, tile, depth, place, *refs):
    panels, column_ref, out_ref, picked = refs[:n], refs[n], refs[n + 1], refs[n + 2]
    y, k = place[0], place[1]
    for d in range(half):
        rows = pl.ds(pl.multiple_of(lax.rem(y + d, n) * tile, tile), tile)
        picked[d * tile:(d + 1) * tile, :depth] = column_ref[rows, depth:]
        picked[d * tile:(d + 1) * tile, depth:] = column_ref[rows, :depth]
    for e in range(n):
        part = lax.dot_general(
            panels[e][...], picked[...], (((1,), (1,)), ((), ())), preferred_element_type=jnp.float32
        )
        m = lax.rem(2 * k - e + n, n)
        for d in range(half):
            out_ref[m, d] = part[:, d * tile:(d + 1) * tile]


def finish(n, half, tile, scale, place, active_ref, own_ref, mirrored_ref, *refs):
    shifted, precision_ref, out_ref = refs[:n - half], refs[n - half], refs[n - half + 1]
    y, k, z = place[0], place[1], place[2]
    row = lax.broadcasted_iota(jnp.int32, (tile, tile), 0)
    column = lax.broadcasted_iota(jnp.int32, (tile, tile), 1)
    for d in range(n):
        t = lax.rem(y + d, n)
        if d == 0:
            total = own_ref[0].T
        elif d < half:
            total = mirrored_ref[d]
        else:
            total = shifted[n - d - 1][...].T
        w = precision_ref[t]
        gradient = total * scale + RIDGE * w
        if d == 0:
            same_tile = lax.rem(2 * k - z + n, n) == 0
            on_diag = (row == column) & same_tile
            inverse = jnp.where(on_diag, 1.0 / jnp.where(on_diag, w, 1.0), 0.0)
            stepped = w - STEP * (gradient - inverse)
        else:
            stepped = w - STEP * gradient
        shrunk = jnp.where(
            stepped > 0, jnp.maximum(stepped - STEP * LASSO, 0.0), jnp.minimum(stepped + STEP * LASSO, 0.0)
        )
        if d == 0:
            shrunk = jnp.where(on_diag, stepped, shrunk)
        out_ref[t] = shrunk * active_ref[t].astype(jnp.float32)


def local(n, resid, samples, precision, active):
    z, y, k = (lax.axis_index(a) for a in AXES)
    place = jnp.stack([y, k, z]).astype(jnp.int32)
    tile, depth = resid.shape
    half = n // 2 + 1

    def moved(a, to):
        ids = [(z * n + y) * n + k for z in range(n) for y in range(n) for k in range(n)]
        ends = []
        for i in ids:
            c = to(i // (n * n), i // n % n, i % n)
            ends.append((c[0] % n * n + c[1] % n) * n + c[2] % n)
        return lax.ppermute(a, AXES, list(zip(ids, ends)))

    own = jnp.concatenate([resid, samples], axis=1)
    column = lax.all_gather(own, "y", axis=0, tiled=True)
    panels = [own] + [moved(own, lambda z, y, k, e=e: (z, y, k + e)) for e in range(1, n)]
    vmem, smem = pl.BlockSpec(memory_space=pltpu.VMEM), pl.BlockSpec(memory_space=pltpu.SMEM)
    partial = pl.pallas_call(
        functools.partial(products, n, half, tile, depth),
        out_shape=jax.ShapeDtypeStruct((n, half, tile, tile), jnp.float32),
        in_specs=[smem] + [vmem] * (n + 1),
        out_specs=vmem,
        scratch_shapes=[pltpu.VMEM((half * tile, 2 * depth), jnp.bfloat16)],
        compiler_params=pltpu.CompilerParams(vmem_limit_bytes=32 * 2**20),
        cost_estimate=pl.CostEstimate(
            flops=4 * n * half * tile * tile * depth, bytes_accessed=8 * 2**20, transcendentals=0
        ),
    )(place, *panels, column)
    summed = lax.psum_scatter(partial, "z", scatter_dimension=0, tiled=True)[0]
    mirrored = moved(summed, lambda z, y, k: (z, y, z - k))
    shifted = [moved(summed[d], lambda z, y, k, d=d: (z, y + d, k)) for d in range(1, n - half + 1)]
    updated = pl.pallas_call(
        functools.partial(finish, n, half, tile, 0.5 / (depth * n)),
        out_shape=jax.ShapeDtypeStruct((n, tile, tile), jnp.float32),
        in_specs=[smem, smem] + [vmem] * (3 + n - half),
        out_specs=vmem,
    )(place, active.reshape(n), summed, mirrored, *shifted, precision.reshape(n, tile, tile))
    return updated.reshape(precision.shape)


def solution(mesh):
    n = mesh.shape["blk"]
    grid = Mesh(mesh.devices.reshape(n, n, n), AXES)
    rows = ("y", "k")
    in_specs = (P(rows, "z"), P(rows, "z"), P(rows, "z"), P(rows, "z"))
    return jax.shard_map(
        functools.partial(local, n), mesh=grid, in_specs=in_specs, out_specs=P(rows, "z"), check_vma=False
    )
```

```python
import functools

import jax
import jax.numpy as jnp
from jax import lax
from jax.experimental import pallas as pl
from jax.experimental.pallas import tpu as pltpu
from jax.sharding import Mesh, PartitionSpec as P

STEP = 1.0
LASSO = 0.1
RIDGE = 0.5
AXES = ("z", "y", "k")
EARLY = (0, 1, 2)
LATE = (5, 4)
CHIP_STEPS = (0, 2, 6, 4)


def products(n, tile, depth, count, place, *refs):
    near, far = refs[:n // 2], refs[n // 2]
    columns, (out_ref, picked) = refs[n // 2 + 1:n // 2 + 1 + count], refs[n // 2 + 1 + count:]
    k = place[1]
    other = k + 1 - 2 * lax.rem(k, 2)
    for i, ref in enumerate(columns):
        picked[i * tile:(i + 1) * tile, :depth] = ref[:, depth:]
        picked[i * tile:(i + 1) * tile, depth:] = ref[:, :depth]
    for e in range(n):
        at = e // 2
        panel = near[at][...] if e % 2 == 0 else far[at * tile:(at + 1) * tile, :]
        home = k if e % 2 == 0 else other
        part = lax.dot_general(panel, picked[...], (((1,), (1,)), ((), ())), preferred_element_type=jnp.float32)
        m = lax.rem(home - CHIP_STEPS[at] + k + n, n)
        for i in range(count):
            out_ref[m, i] = part[:, i * tile:(i + 1) * tile]


def finish(n, tile, scale, place, active_ref, *refs):
    own, early, late, one, two, three, precision_ref, out_ref = refs
    y, k, z = place[0], place[1], place[2]
    row = lax.broadcasted_iota(jnp.int32, (tile, tile), 0)
    column = lax.broadcasted_iota(jnp.int32, (tile, tile), 1)
    found = (
        lambda: own[0].T, lambda: early[1], lambda: early[2], lambda: three[...].T,
        lambda: late[1], lambda: late[0], lambda: two[...].T, lambda: one[...].T,
    )
    for d in range(n):
        t = lax.rem(y + d, n)
        w = precision_ref[t]
        gradient = found[d]() * scale + RIDGE * w
        if d == 0:
            same_tile = lax.rem(2 * k - z + n, n) == 0
            on_diag = (row == column) & same_tile
            inverse = jnp.where(on_diag, 1.0 / jnp.where(on_diag, w, 1.0), 0.0)
            stepped = w - STEP * (gradient - inverse)
        else:
            stepped = w - STEP * gradient
        shrunk = jnp.where(
            stepped > 0, jnp.maximum(stepped - STEP * LASSO, 0.0), jnp.minimum(stepped + STEP * LASSO, 0.0)
        )
        if d == 0:
            shrunk = jnp.where(on_diag, stepped, shrunk)
        out_ref[t] = shrunk * active_ref[t].astype(jnp.float32)


def added(ref, out_ref):
    out_ref[...] = jnp.sum(ref[...], axis=0)


def local(n, resid, samples, precision, active):
    z, y, k = (lax.axis_index(a) for a in AXES)
    place = jnp.stack([y, k, z]).astype(jnp.int32)
    tile, depth = resid.shape
    vmem, smem = pl.BlockSpec(memory_space=pltpu.VMEM), pl.BlockSpec(memory_space=pltpu.SMEM)

    def moved(a, to):
        ids = [(z * n + y) * n + k for z in range(n) for y in range(n) for k in range(n)]
        ends = []
        for i in ids:
            c = to(i // (n * n), i // n % n, i % n)
            ends.append((c[0] % n * n + c[1] % n) * n + c[2] % n)
        return lax.ppermute(a, AXES, list(zip(ids, ends)))

    def multiplied(near, far, columns):
        count = len(columns)
        return pl.pallas_call(
            functools.partial(products, n, tile, depth, count),
            out_shape=jax.ShapeDtypeStruct((n, count, tile, tile), jnp.float32),
            in_specs=[smem] + [vmem] * (n // 2 + 1 + count),
            out_specs=vmem,
            scratch_shapes=[pltpu.VMEM((count * tile, 2 * depth), jnp.bfloat16)],
            compiler_params=pltpu.CompilerParams(vmem_limit_bytes=32 * 2**20),
            cost_estimate=pl.CostEstimate(
                flops=4 * n * count * tile * tile * depth, bytes_accessed=4 * 2**20, transcendentals=0
            ),
        )(place, *near, far, *columns)

    own = jnp.concatenate([resid, samples], axis=1)
    near = [own] + [moved(own, lambda z, y, k, s=s: (z, y, k + s)) for s in CHIP_STEPS[1:]]
    panel = {d: moved(own, lambda z, y, k, d=d: (z, y - d, k)) for d in (1, 2, 5, 4)}
    panel[0] = own
    far = moved(jnp.concatenate(near, axis=0), lambda z, y, k: (z, y, k ^ 1))
    early = lax.psum_scatter(
        multiplied(near, far, [panel[d] for d in EARLY]), "z", scatter_dimension=0, tiled=True
    )[0]
    parts = lax.all_to_all(multiplied(near, far, [panel[d] for d in LATE]), "z", 0, 0, tiled=True)
    late = pl.pallas_call(
        added, out_shape=jax.ShapeDtypeStruct(parts.shape[1:], jnp.float32), in_specs=[vmem], out_specs=vmem
    )(parts)
    three = moved(late[0], lambda z, y, k: (z, y + 5, k))
    late = moved(late, lambda z, y, k: (z, y, z - k))
    one = moved(early[1], lambda z, y, k: (z, y + 1, k))
    two = moved(early[2], lambda z, y, k: (z, y + 2, k))
    mirrored = moved(early, lambda z, y, k: (z, y, z - k))
    updated = pl.pallas_call(
        functools.partial(finish, n, tile, 0.5 / (depth * n)),
        out_shape=jax.ShapeDtypeStruct((n, tile, tile), jnp.float32),
        in_specs=[smem, smem] + [vmem] * 7,
        out_specs=vmem,
    )(place, active.reshape(n), early, mirrored, late, one, two, three, precision.reshape(n, tile, tile))
    return updated.reshape(precision.shape)


def solution(mesh):
    n = mesh.shape["blk"]
    grid = Mesh(mesh.devices.reshape(n, n, n), AXES)
    rows = ("y", "k")
    in_specs = (P(rows, "z"), P(rows, "z"), P(rows, "z"), P(rows, "z"))
    return jax.shard_map(
        functools.partial(local, n), mesh=grid, in_specs=in_specs, out_specs=P(rows, "z"), check_vma=False
    )
```

```python
import functools

import jax
import jax.numpy as jnp
from jax import lax
from jax.experimental import pallas as pl
from jax.experimental.pallas import tpu as pltpu
from jax.sharding import Mesh, PartitionSpec as P

STEP = 1.0
LASSO = 0.1
RIDGE = 0.5
AXES = ("z", "y", "k")
DIRECT = (0, 7, 2, 3, 4)
TURNED = (1, 2, 3)


def products(tile, depth, place, panel, *refs):
    columns, (out_ref, picked) = refs[:-2], refs[-2:]

    @pl.when(pl.program_id(0) == 0)
    def _():
        for i, ref in enumerate(columns):
            picked[i * tile:(i + 1) * tile, :depth] = ref[:, depth:]
            picked[i * tile:(i + 1) * tile, depth:] = ref[:, :depth]

    part = lax.dot_general(panel[...], picked[...], (((1,), (1,)), ((), ())), preferred_element_type=jnp.float32)
    for i in range(len(columns)):
        out_ref[0, i] = part[:, i * tile:(i + 1) * tile]


def proximal(total, w, scale, inverse=0.0):
    stepped = w - STEP * (total * scale + RIDGE * w - inverse)
    shrunk = jnp.where(
        stepped > 0, jnp.maximum(stepped - STEP * LASSO, 0.0), jnp.minimum(stepped + STEP * LASSO, 0.0)
    )
    return stepped, shrunk


def finish_direct(n, tile, scale, place, active_ref, summed, precision_ref, out_ref):
    y, k, z = place[0], place[1], place[2]
    row = lax.broadcasted_iota(jnp.int32, (tile, tile), 0)
    column = lax.broadcasted_iota(jnp.int32, (tile, tile), 1)
    for i, d in enumerate(DIRECT):
        t = lax.rem(y + d, n)
        w = precision_ref[t]
        if d == 0:
            on_diag = (row == column) & (lax.rem(2 * k - z + n, n) == 0)
            inverse = jnp.where(on_diag, 1.0 / jnp.where(on_diag, w, 1.0), 0.0)
            stepped, shrunk = proximal(summed[i], w, scale, inverse)
            shrunk = jnp.where(on_diag, stepped, shrunk)
        else:
            _, shrunk = proximal(summed[i], w, scale)
        out_ref[t] = shrunk * active_ref[t].astype(jnp.float32)


def finish_turned(n, scale, place, active_ref, *refs):
    arrived, (precision_ref, _, out_ref) = refs[:-3], refs[-3:]
    for i, a in enumerate(arrived):

        @pl.when(pl.program_id(0) == i)
        def _(a=a, d=n - DIRECT[TURNED[i]]):
            t = lax.rem(place[0] + d, n)
            _, shrunk = proximal(a[...].T, precision_ref[0], scale)
            out_ref[0] = shrunk * active_ref[t].astype(jnp.float32)


def local(n, resid, samples, precision, active):
    z, y, k = (lax.axis_index(a) for a in AXES)
    place = jnp.stack([y, k, z]).astype(jnp.int32)
    tile, depth = resid.shape
    vmem, smem = pl.BlockSpec(memory_space=pltpu.VMEM), pl.BlockSpec(memory_space=pltpu.SMEM)

    def index(z, y, k):
        return (z % n * n + y % n) * n + k % n

    def moved(a, to):
        ids = [(z, y, k) for z in range(n) for y in range(n) for k in range(n)]
        return lax.ppermute(a, AXES, [(index(*i), index(*to(*i))) for i in ids])

    own = jnp.concatenate([resid, samples], axis=1)
    rows = lax.all_gather(own, "k", axis=0, tiled=True)
    columns = [moved(own, lambda z, y, k, d=d: (z, y - d, z - k)) for d in DIRECT]
    whole = pl.BlockSpec((tile, 2 * depth), lambda e, place: (0, 0))
    partial = pl.pallas_call(
        functools.partial(products, tile, depth),
        out_shape=jax.ShapeDtypeStruct((n, len(DIRECT), tile, tile), jnp.float32),
        grid_spec=pltpu.PrefetchScalarGridSpec(
            num_scalar_prefetch=1,
            grid=(n,),
            in_specs=[pl.BlockSpec((tile, 2 * depth), lambda e, place: (e, 0))] + [whole] * len(DIRECT),
            out_specs=pl.BlockSpec(
                (1, len(DIRECT), tile, tile),
                lambda e, place: (lax.rem(e + place[2] - place[1] + n, n), 0, 0, 0),
            ),
            scratch_shapes=[pltpu.VMEM((len(DIRECT) * tile, 2 * depth), jnp.bfloat16)],
        ),
        compiler_params=pltpu.CompilerParams(vmem_limit_bytes=60 * 2**20),
        cost_estimate=pl.CostEstimate(
            flops=4 * n * len(DIRECT) * tile * tile * depth, bytes_accessed=5 * 2**20, transcendentals=0
        ),
    )(place, rows, *columns)
    diagonals = [[index(z, y, z - k) for z in range(n)] for y in range(n) for k in range(n)]
    summed = lax.psum_scatter(partial, AXES, scatter_dimension=0, axis_index_groups=diagonals, tiled=True)[0]
    arrived = [
        moved(summed[i], lambda z, y, k, d=DIRECT[i]: (z, y + d, z - k)) for i in TURNED
    ]
    scale = 0.5 / (depth * n)
    flags, tiles = active.reshape(n), precision.reshape(n, tile, tile)
    updated = pl.pallas_call(
        functools.partial(finish_direct, n, tile, scale),
        out_shape=jax.ShapeDtypeStruct((n, tile, tile), jnp.float32),
        in_specs=[smem, smem, vmem, vmem],
        out_specs=vmem,
    )(place, flags, summed, tiles)

    def turned_tile(i, place, flags):
        d = jnp.where(i == 0, n - DIRECT[TURNED[0]], jnp.where(i == 1, n - DIRECT[TURNED[1]], n - DIRECT[TURNED[2]]))
        return lax.rem(place[0] + d, n), 0, 0

    one = pl.BlockSpec((1, tile, tile), turned_tile)
    updated = pl.pallas_call(
        functools.partial(finish_turned, n, scale),
        out_shape=jax.ShapeDtypeStruct((n, tile, tile), jnp.float32),
        grid_spec=pltpu.PrefetchScalarGridSpec(
            num_scalar_prefetch=2,
            grid=(len(TURNED),),
            in_specs=[pl.BlockSpec((tile, tile), lambda i, place, flags: (0, 0))] * len(TURNED)
            + [one, pl.BlockSpec(memory_space=pl.ANY)],
            out_specs=one,
        ),
        input_output_aliases={3 + len(TURNED): 0},
    )(place, flags, *arrived, tiles, updated)
    return updated.reshape(precision.shape)


def solution(mesh):
    n = mesh.shape["blk"]
    grid = Mesh(mesh.devices.reshape(n, n, n), AXES)
    rows = ("y", "k")
    in_specs = (P(rows, "z"), P(rows, "z"), P(rows, "z"), P(rows, "z"))
    return jax.shard_map(
        functools.partial(local, n), mesh=grid, in_specs=in_specs, out_specs=P(rows, "z"), check_vma=False
    )
```

```python
import functools

import jax
import jax.numpy as jnp
from jax import lax
from jax.experimental import pallas as pl
from jax.experimental.pallas import tpu as pltpu
from jax.sharding import Mesh, PartitionSpec as P

STEP = 1.0
LASSO = 0.1
RIDGE = 0.5
AXES = ("z", "y", "k")
OFFSETS = (0, 7, 2, 3, 4)
TURNED = (1, 2, 3)
CHUNKS = 4
MIB = 2**20


def join(a_ref, b_ref, out_ref):
    half = a_ref.shape[1]
    out_ref[:, :half] = a_ref[...]
    out_ref[:, half:] = b_ref[...]


def products(n, tile, depth, rows_ref, *refs):
    count = len(OFFSETS)
    columns, (out_ref, rows, picked, made, row_sems, column_sems, out_sems) = refs[:count], refs[count:]
    k = lax.axis_index("k")
    per = n // CHUNKS
    loads = []
    for i, ref in enumerate(columns):
        at = pl.ds(i * tile, tile)
        for h in range(2):
            here, there = pl.ds(h * depth, depth), pl.ds((1 - h) * depth, depth)
            loads.append(pltpu.make_async_copy(ref.at[:, there], picked.at[at, here], column_sems.at[i, h]))
    chunks = [
        pltpu.make_async_copy(rows_ref.at[pl.ds(c * per * tile, per * tile)], rows.at[c], row_sems.at[c])
        for c in range(CHUNKS)
    ]
    for copy in loads + chunks:
        copy.start()
    for copy in loads:
        copy.wait()
    stores = []
    for c in range(CHUNKS):
        chunks[c].wait()
        part = lax.dot_general(
            rows[c], picked[...], (((1,), (1,)), ((), ())), preferred_element_type=jnp.float32
        )
        for e in range(per):
            j = c * per + e
            for i in range(count):
                made[j, i] = part[e * tile:(e + 1) * tile, i * tile:(i + 1) * tile]
            m = lax.rem(j + k, n)
            stores.append(pltpu.make_async_copy(made.at[j], out_ref.at[m], out_sems.at[j]))
            stores[-1].start()
    for copy in stores:
        copy.wait()


def finish(n, tile, scale, active_ref, own, mirrored, *refs):
    arrived, (precision_ref, out_ref) = refs[:-2], refs[-2:]
    z, y, k = (lax.axis_index(a) for a in AXES)
    row = lax.broadcasted_iota(jnp.int32, (tile, tile), 0)
    column = lax.broadcasted_iota(jnp.int32, (tile, tile), 1)

    def put(d, total):
        t = lax.rem(y + d, n)
        w = precision_ref[t]
        gradient = total * scale + RIDGE * w
        if d == 0:
            on_diag = (row == column) & (lax.rem(2 * k - z + n, n) == 0)
            inverse = jnp.where(on_diag, 1.0 / jnp.where(on_diag, w, 1.0), 0.0)
            stepped = w - STEP * (gradient - inverse)
        else:
            stepped = w - STEP * gradient
        shrunk = jnp.where(
            stepped > 0, jnp.maximum(stepped - STEP * LASSO, 0.0), jnp.minimum(stepped + STEP * LASSO, 0.0)
        )
        if d == 0:
            shrunk = jnp.where(on_diag, stepped, shrunk)
        out_ref[t] = shrunk * active_ref[t].astype(jnp.float32)

    put(0, own[0].T)
    for i in range(1, len(OFFSETS)):
        put(OFFSETS[i], mirrored[i])
    for i, ref in zip(TURNED, arrived):
        put(n - OFFSETS[i], ref[...].T)


def local(n, resid, samples, precision, active):
    tile, depth = resid.shape
    vmem, smem, anywhere = (pl.BlockSpec(memory_space=s) for s in (pltpu.VMEM, pltpu.SMEM, pl.ANY))
    count = len(OFFSETS)

    def moved(a, to):
        def index(z, y, k):
            return (z % n * n + y % n) * n + k % n

        ids = [(z, y, k) for z in range(n) for y in range(n) for k in range(n)]
        return lax.ppermute(a, AXES, [(index(*i), index(*to(*i))) for i in ids])

    own = pl.pallas_call(
        join,
        out_shape=jax.ShapeDtypeStruct((tile, 2 * depth), resid.dtype),
        in_specs=[vmem, vmem],
        out_specs=vmem,
        compiler_params=pltpu.CompilerParams(vmem_limit_bytes=60 * MIB),
    )(resid, samples)
    rows = lax.all_gather(own, "k", axis=0, tiled=True)
    columns = [own] + [moved(own, lambda z, y, k, d=d: (z, y - d, k)) for d in OFFSETS[1:]]
    partial = pl.pallas_call(
        functools.partial(products, n, tile, depth),
        out_shape=jax.ShapeDtypeStruct((n, count, tile, tile), jnp.float32),
        in_specs=[anywhere] * (1 + count),
        out_specs=anywhere,
        scratch_shapes=[
            pltpu.VMEM((CHUNKS, n // CHUNKS * tile, 2 * depth), jnp.bfloat16),
            pltpu.VMEM((count * tile, 2 * depth), jnp.bfloat16),
            pltpu.VMEM((n, count, tile, tile), jnp.float32),
            pltpu.SemaphoreType.DMA((CHUNKS,)),
            pltpu.SemaphoreType.DMA((count, 2)),
            pltpu.SemaphoreType.DMA((n,)),
        ],
        compiler_params=pltpu.CompilerParams(vmem_limit_bytes=60 * MIB),
        cost_estimate=pl.CostEstimate(
            flops=4 * n * count * tile * tile * depth, bytes_accessed=6 * MIB, transcendentals=0
        ),
    )(rows, *columns)
    summed = lax.psum_scatter(partial, "z", scatter_dimension=0, tiled=True)[0]
    mirrored = moved(summed, lambda z, y, k: (z, y, z - k))
    arrived = [moved(summed[i], lambda z, y, k, d=OFFSETS[i]: (z, y + d, k)) for i in TURNED]
    updated = pl.pallas_call(
        functools.partial(finish, n, tile, 0.5 / (depth * n)),
        out_shape=jax.ShapeDtypeStruct((n, tile, tile), jnp.float32),
        in_specs=[smem] + [vmem] * (3 + len(TURNED)),
        out_specs=vmem,
        compiler_params=pltpu.CompilerParams(vmem_limit_bytes=16 * MIB),
    )(active.reshape(n), summed, mirrored, *arrived, precision.reshape(n, tile, tile))
    return updated.reshape(precision.shape)


def solution(mesh):
    n = mesh.shape["blk"]
    grid = Mesh(mesh.devices.reshape(n, n, n), AXES)
    rows = ("y", "k")
    in_specs = (P(rows, "z"), P(rows, "z"), P(rows, "z"), P(rows, "z"))
    return jax.shard_map(
        functools.partial(local, n), mesh=grid, in_specs=in_specs, out_specs=P(rows, "z"), check_vma=False
    )
```

```python
import functools

import jax
import jax.numpy as jnp
from jax import lax
from jax.experimental import pallas as pl
from jax.experimental.pallas import tpu as pltpu
from jax.sharding import Mesh, PartitionSpec as P

STEP = 1.0
LASSO = 0.1
RIDGE = 0.5
AXES = ("z", "y", "k")
EARLY = (0, 7, 4)
LATE = (2, 3)
CHUNKS = 4
MIB = 2**20


def join(a_ref, b_ref, out_ref):
    half = a_ref.shape[1]
    out_ref[:, :half] = a_ref[...]
    out_ref[:, half:] = b_ref[...]


def products(n, tile, depth, count, rows_ref, *refs):
    columns, (out_ref, rows, picked, made, row_sems, column_sems, out_sems) = refs[:count], refs[count:]
    k = lax.axis_index("k")
    per = n // CHUNKS
    loads = []
    for i, ref in enumerate(columns):
        at = pl.ds(i * tile, tile)
        for h in range(2):
            here, there = pl.ds(h * depth, depth), pl.ds((1 - h) * depth, depth)
            loads.append(pltpu.make_async_copy(ref.at[:, there], picked.at[at, here], column_sems.at[i, h]))
    chunks = [
        pltpu.make_async_copy(rows_ref.at[pl.ds(c * per * tile, per * tile)], rows.at[c], row_sems.at[c])
        for c in range(CHUNKS)
    ]
    for copy in loads + chunks:
        copy.start()
    for copy in loads:
        copy.wait()
    stores = []
    for c in range(CHUNKS):
        chunks[c].wait()
        part = lax.dot_general(
            rows[c], picked[...], (((1,), (1,)), ((), ())), preferred_element_type=jnp.float32
        )
        for e in range(per):
            j = c * per + e
            for i in range(count):
                made[j, i] = part[e * tile:(e + 1) * tile, i * tile:(i + 1) * tile]
            m = lax.rem(j + k, n)
            stores.append(pltpu.make_async_copy(made.at[j], out_ref.at[m], out_sems.at[j]))
            stores[-1].start()
    for copy in stores:
        copy.wait()


def added(parts_ref, out_ref, *each):
    for i, ref in enumerate(each):
        total = jnp.sum(parts_ref[:, i], axis=0)
        out_ref[i] = total
        ref[...] = total


def finish(n, tile, scale, active_ref, own, early, late, *refs):
    arrived, (precision_ref, out_ref) = refs[:-2], refs[-2:]
    z, y, k = (lax.axis_index(a) for a in AXES)
    row = lax.broadcasted_iota(jnp.int32, (tile, tile), 0)
    column = lax.broadcasted_iota(jnp.int32, (tile, tile), 1)

    def put(d, total):
        t = lax.rem(y + d, n)
        w = precision_ref[t]
        gradient = total * scale + RIDGE * w
        if d == 0:
            on_diag = (row == column) & (lax.rem(2 * k - z + n, n) == 0)
            inverse = jnp.where(on_diag, 1.0 / jnp.where(on_diag, w, 1.0), 0.0)
            stepped = w - STEP * (gradient - inverse)
        else:
            stepped = w - STEP * gradient
        shrunk = jnp.where(
            stepped > 0, jnp.maximum(stepped - STEP * LASSO, 0.0), jnp.minimum(stepped + STEP * LASSO, 0.0)
        )
        if d == 0:
            shrunk = jnp.where(on_diag, stepped, shrunk)
        out_ref[t] = shrunk * active_ref[t].astype(jnp.float32)

    put(0, own[0].T)
    for i in range(1, len(EARLY)):
        put(EARLY[i], early[i])
    for i in range(len(LATE)):
        put(LATE[i], late[i])
    for d, ref in zip((EARLY[1],) + LATE, arrived):
        put(n - d, ref[...].T)


def local(n, resid, samples, precision, active):
    tile, depth = resid.shape
    vmem, smem, anywhere = (pl.BlockSpec(memory_space=s) for s in (pltpu.VMEM, pltpu.SMEM, pl.ANY))

    def moved(a, to):
        def index(z, y, k):
            return (z % n * n + y % n) * n + k % n

        ids = [(z, y, k) for z in range(n) for y in range(n) for k in range(n)]
        return lax.ppermute(a, AXES, [(index(*i), index(*to(*i))) for i in ids])

    def multiplied(rows, columns, flops):
        count = len(columns)
        return pl.pallas_call(
            functools.partial(products, n, tile, depth, count),
            out_shape=jax.ShapeDtypeStruct((n, count, tile, tile), jnp.float32),
            in_specs=[anywhere] * (1 + count),
            out_specs=anywhere,
            scratch_shapes=[
                pltpu.VMEM((CHUNKS, n // CHUNKS * tile, 2 * depth), jnp.bfloat16),
                pltpu.VMEM((count * tile, 2 * depth), jnp.bfloat16),
                pltpu.VMEM((n, count, tile, tile), jnp.float32),
                pltpu.SemaphoreType.DMA((CHUNKS,)),
                pltpu.SemaphoreType.DMA((count, 2)),
                pltpu.SemaphoreType.DMA((n,)),
            ],
            compiler_params=pltpu.CompilerParams(vmem_limit_bytes=60 * MIB),
            cost_estimate=pl.CostEstimate(flops=flops, bytes_accessed=4 * MIB, transcendentals=0),
        )(rows, *columns)

    own = pl.pallas_call(
        join,
        out_shape=jax.ShapeDtypeStruct((tile, 2 * depth), resid.dtype),
        in_specs=[vmem, vmem],
        out_specs=vmem,
        compiler_params=pltpu.CompilerParams(vmem_limit_bytes=60 * MIB),
    )(resid, samples)
    rows = lax.all_gather(own, "k", axis=0, tiled=True)
    panel = {d: moved(own, lambda z, y, k, d=d: (z, y - d, k)) for d in EARLY[1:] + LATE}
    panel[0] = own
    once = 4 * n * tile * tile * depth
    early = lax.psum_scatter(
        multiplied(rows, [panel[d] for d in EARLY], once), "z", scatter_dimension=0, tiled=True
    )[0]
    weight = 600 * once
    parts = lax.all_to_all(multiplied(rows, [panel[d] for d in LATE], weight), "z", 0, 0, tiled=True)
    square = jax.ShapeDtypeStruct((tile, tile), jnp.float32)
    late, *each = pl.pallas_call(
        added,
        out_shape=[jax.ShapeDtypeStruct((len(LATE), tile, tile), jnp.float32)] + [square] * len(LATE),
        in_specs=[vmem],
        out_specs=[vmem] * (1 + len(LATE)),
        compiler_params=pltpu.CompilerParams(vmem_limit_bytes=16 * MIB),
    )(parts)
    late = moved(late, lambda z, y, k: (z, y, z - k))
    arrived = [moved(a, lambda z, y, k, d=d: (z, y + d, k)) for a, d in zip(each, LATE)]
    arrived = [moved(early[1], lambda z, y, k: (z, y + EARLY[1], k))] + arrived
    mirrored = moved(early, lambda z, y, k: (z, y, z - k))
    updated = pl.pallas_call(
        functools.partial(finish, n, tile, 0.5 / (depth * n)),
        out_shape=jax.ShapeDtypeStruct((n, tile, tile), jnp.float32),
        in_specs=[smem] + [vmem] * (4 + len(arrived)),
        out_specs=vmem,
        compiler_params=pltpu.CompilerParams(vmem_limit_bytes=16 * MIB),
    )(active.reshape(n), early, mirrored, late, *arrived, precision.reshape(n, tile, tile))
    return updated.reshape(precision.shape)


def solution(mesh):
    n = mesh.shape["blk"]
    grid = Mesh(mesh.devices.reshape(n, n, n), AXES)
    rows = ("y", "k")
    in_specs = (P(rows, "z"), P(rows, "z"), P(rows, "z"), P(rows, "z"))
    return jax.shard_map(
        functools.partial(local, n), mesh=grid, in_specs=in_specs, out_specs=P(rows, "z"), check_vma=False
    )
```

```python
import functools

import jax
import jax.numpy as jnp
from jax import lax
from jax.experimental import pallas as pl
from jax.experimental.pallas import tpu as pltpu
from jax.sharding import Mesh, PartitionSpec as P

STEP = 1.0
LASSO = 0.1
RIDGE = 0.5
AXES = ("z", "y", "k")
OFFSETS = (0, 7, 6, 3, 4)
TURNED = (1, 2, 3)
CHUNKS = 4
MIB = 2**20


def join(a_ref, b_ref, out_ref):
    half = a_ref.shape[1]
    out_ref[:, :half] = a_ref[...]
    out_ref[:, half:] = b_ref[...]


def products(n, tile, depth, rows_ref, *refs):
    count = len(OFFSETS)
    columns, (out_ref, rows, picked, made, row_sems, column_sems, out_sems) = refs[:count], refs[count:]
    k = lax.axis_index("k")
    per = n // CHUNKS
    loads = []
    for i, ref in enumerate(columns):
        at = pl.ds(i * tile, tile)
        for h in range(2):
            here, there = pl.ds(h * depth, depth), pl.ds((1 - h) * depth, depth)
            loads.append(pltpu.make_async_copy(ref.at[:, there], picked.at[at, here], column_sems.at[i, h]))
    chunks = [
        pltpu.make_async_copy(rows_ref.at[pl.ds(c * per * tile, per * tile)], rows.at[c], row_sems.at[c])
        for c in range(CHUNKS)
    ]
    for copy in loads + chunks:
        copy.start()
    for copy in loads:
        copy.wait()
    stores = []
    for c in range(CHUNKS):
        chunks[c].wait()
        part = lax.dot_general(
            rows[c], picked[...], (((1,), (1,)), ((), ())), preferred_element_type=jnp.float32
        )
        for e in range(per):
            j = c * per + e
            for i in range(count):
                made[j, i] = part[e * tile:(e + 1) * tile, i * tile:(i + 1) * tile]
            m = lax.rem(j + k, n)
            stores.append(pltpu.make_async_copy(made.at[j], out_ref.at[m], out_sems.at[j]))
            stores[-1].start()
    for copy in stores:
        copy.wait()


def finish(n, tile, scale, active_ref, own, mirrored, *refs):
    arrived, (precision_ref, out_ref) = refs[:-2], refs[-2:]
    z, y, k = (lax.axis_index(a) for a in AXES)
    row = lax.broadcasted_iota(jnp.int32, (tile, tile), 0)
    column = lax.broadcasted_iota(jnp.int32, (tile, tile), 1)

    def put(d, total):
        t = lax.rem(y + d, n)
        w = precision_ref[t]
        gradient = total * scale + RIDGE * w
        if d == 0:
            on_diag = (row == column) & (lax.rem(2 * k - z + n, n) == 0)
            inverse = jnp.where(on_diag, 1.0 / jnp.where(on_diag, w, 1.0), 0.0)
            stepped = w - STEP * (gradient - inverse)
        else:
            stepped = w - STEP * gradient
        shrunk = jnp.where(
            stepped > 0, jnp.maximum(stepped - STEP * LASSO, 0.0), jnp.minimum(stepped + STEP * LASSO, 0.0)
        )
        if d == 0:
            shrunk = jnp.where(on_diag, stepped, shrunk)
        out_ref[t] = shrunk * active_ref[t].astype(jnp.float32)

    put(0, own[...].T)
    for i in range(1, len(OFFSETS)):
        put(OFFSETS[i], mirrored[i])
    for i, ref in zip(TURNED, arrived):
        put(n - OFFSETS[i], ref[...].T)


def local(n, resid, samples, precision, active):
    tile, depth = resid.shape
    vmem, smem, anywhere = (pl.BlockSpec(memory_space=s) for s in (pltpu.VMEM, pltpu.SMEM, pl.ANY))
    count = len(OFFSETS)

    def moved(a, to):
        def index(z, y, k):
            return (z % n * n + y % n) * n + k % n

        ids = [(z, y, k) for z in range(n) for y in range(n) for k in range(n)]
        return lax.ppermute(a, AXES, [(index(*i), index(*to(*i))) for i in ids])

    own = pl.pallas_call(
        join,
        out_shape=jax.ShapeDtypeStruct((tile, 2 * depth), resid.dtype),
        in_specs=[vmem, vmem],
        out_specs=vmem,
        compiler_params=pltpu.CompilerParams(vmem_limit_bytes=60 * MIB),
    )(resid, samples)
    rows = lax.all_gather(own, "k", axis=0, tiled=True)
    columns = [own] + [moved(own, lambda z, y, k, d=d: (z, y - d, k)) for d in OFFSETS[1:]]
    partial = pl.pallas_call(
        functools.partial(products, n, tile, depth),
        out_shape=jax.ShapeDtypeStruct((n, count, tile, tile), jnp.float32),
        in_specs=[anywhere] * (1 + count),
        out_specs=anywhere,
        scratch_shapes=[
            pltpu.VMEM((CHUNKS, n // CHUNKS * tile, 2 * depth), jnp.bfloat16),
            pltpu.VMEM((count * tile, 2 * depth), jnp.bfloat16),
            pltpu.VMEM((n, count, tile, tile), jnp.float32),
            pltpu.SemaphoreType.DMA((CHUNKS,)),
            pltpu.SemaphoreType.DMA((count, 2)),
            pltpu.SemaphoreType.DMA((n,)),
        ],
        compiler_params=pltpu.CompilerParams(vmem_limit_bytes=60 * MIB),
        cost_estimate=pl.CostEstimate(
            flops=4 * n * count * tile * tile * depth, bytes_accessed=6 * MIB, transcendentals=0
        ),
    )(rows, *columns)
    summed = lax.psum_scatter(partial, "z", scatter_dimension=0, tiled=True)[0]
    mirrored = moved(summed, lambda z, y, k: (z, y, z - k))
    arrived = [moved(summed[i], lambda z, y, k, d=OFFSETS[i]: (z, y + d, k)) for i in TURNED]
    updated = pl.pallas_call(
        functools.partial(finish, n, tile, 0.5 / (depth * n)),
        out_shape=jax.ShapeDtypeStruct((n, tile, tile), jnp.float32),
        in_specs=[smem] + [vmem] * (3 + len(TURNED)),
        out_specs=vmem,
        compiler_params=pltpu.CompilerParams(vmem_limit_bytes=16 * MIB),
    )(active.reshape(n), summed[0], mirrored, *arrived, precision.reshape(n, tile, tile))
    return updated.reshape(precision.shape)


def solution(mesh):
    n = mesh.shape["blk"]
    grid = Mesh(mesh.devices.reshape(n, n, n), AXES)
    rows = ("y", "k")
    in_specs = (P(rows, "z"), P(rows, "z"), P(rows, "z"), P(rows, "z"))
    return jax.shard_map(
        functools.partial(local, n), mesh=grid, in_specs=in_specs, out_specs=P(rows, "z"), check_vma=False
    )
```

```python
import functools

import jax
import jax.numpy as jnp
from jax import lax
from jax.experimental import pallas as pl
from jax.experimental.pallas import tpu as pltpu
from jax.sharding import Mesh, PartitionSpec as P

STEP = 1.0
LASSO = 0.1
RIDGE = 0.5
AXES = ("z", "y", "k")
OFFSETS = (0, 7, 6, 4, 3)
TURNED = (1, 2, 4)
CHUNKS = 2
MIB = 2**20


def join(a_ref, b_ref, out_ref):
    half = a_ref.shape[1]
    out_ref[:, :half] = a_ref[...]
    out_ref[:, half:] = b_ref[...]


def products(n, tile, depth, rows_ref, *refs):
    count = len(OFFSETS)
    columns, (out_ref, rows, picked, made, own_sems, row_sems, out_sems) = refs[:count - 1], refs[count - 1:]
    k = lax.axis_index("k")
    per = n // CHUNKS
    chunks = [
        pltpu.make_async_copy(rows_ref.at[pl.ds(c * per * tile, per * tile)], rows.at[c], row_sems.at[c])
        for c in range(CHUNKS)
    ]
    here = [
        pltpu.make_async_copy(
            rows_ref.at[pl.ds(pl.multiple_of(k * tile, tile), tile), pl.ds((1 - h) * depth, depth)],
            picked.at[pl.ds(0, tile), pl.ds(h * depth, depth)],
            own_sems.at[h],
        )
        for h in range(2)
    ]
    for copy in here + chunks:
        copy.start()
    for i, ref in enumerate(columns, 1):
        picked[i * tile:(i + 1) * tile, :depth] = ref[:, depth:]
        picked[i * tile:(i + 1) * tile, depth:] = ref[:, :depth]
    for copy in here:
        copy.wait()
    stores = []
    for c in range(CHUNKS):
        chunks[c].wait()
        part = lax.dot_general(
            rows[c], picked[...], (((1,), (1,)), ((), ())), preferred_element_type=jnp.float32
        )
        for e in range(per):
            j = c * per + e
            for i in range(count):
                made[j, i] = part[e * tile:(e + 1) * tile, i * tile:(i + 1) * tile]
            m = lax.rem(j + k, n)
            stores.append(pltpu.make_async_copy(made.at[j], out_ref.at[m], out_sems.at[j]))
            stores[-1].start()
    for copy in stores:
        copy.wait()


def finish(n, tile, scale, active_ref, mirrored, *refs):
    arrived, (precision_ref, out_ref) = refs[:-2], refs[-2:]
    z, y, k = (lax.axis_index(a) for a in AXES)
    row = lax.broadcasted_iota(jnp.int32, (tile, tile), 0)
    column = lax.broadcasted_iota(jnp.int32, (tile, tile), 1)

    def put(d, total):
        t = lax.rem(y + d, n)
        w = precision_ref[t]
        gradient = total * scale + RIDGE * w
        if d == 0:
            on_diag = (row == column) & (lax.rem(2 * k - z + n, n) == 0)
            inverse = jnp.where(on_diag, 1.0 / jnp.where(on_diag, w, 1.0), 0.0)
            stepped = w - STEP * (gradient - inverse)
        else:
            stepped = w - STEP * gradient
        shrunk = jnp.where(
            stepped > 0, jnp.maximum(stepped - STEP * LASSO, 0.0), jnp.minimum(stepped + STEP * LASSO, 0.0)
        )
        if d == 0:
            shrunk = jnp.where(on_diag, stepped, shrunk)
        out_ref[t] = shrunk * active_ref[t].astype(jnp.float32)

    for i, d in enumerate(OFFSETS):
        put(d, mirrored[i])
    for i, ref in zip(TURNED, arrived):
        put(n - OFFSETS[i], ref[...].T)


def local(n, resid, samples, precision, active):
    tile, depth = resid.shape
    vmem, smem, far = (pl.BlockSpec(memory_space=s) for s in (pltpu.VMEM, pltpu.SMEM, pltpu.HBM))
    count = len(OFFSETS)

    def moved(a, to):
        def index(z, y, k):
            return (z % n * n + y % n) * n + k % n

        ids = [(z, y, k) for z in range(n) for y in range(n) for k in range(n)]
        return lax.ppermute(a, AXES, [(index(*i), index(*to(*i))) for i in ids])

    own = pl.pallas_call(
        join,
        out_shape=jax.ShapeDtypeStruct((tile, 2 * depth), resid.dtype),
        in_specs=[vmem, vmem],
        out_specs=vmem,
        compiler_params=pltpu.CompilerParams(vmem_limit_bytes=60 * MIB),
    )(resid, samples)
    rows = lax.all_gather(own, "k", axis=0, tiled=True)
    columns = [moved(own, lambda z, y, k, d=d: (z, y - d, k)) for d in OFFSETS[1:]]
    partial = pl.pallas_call(
        functools.partial(products, n, tile, depth),
        out_shape=jax.ShapeDtypeStruct((n, count, tile, tile), jnp.float32),
        in_specs=[far] + [vmem] * (count - 1),
        out_specs=far,
        scratch_shapes=[
            pltpu.VMEM((CHUNKS, n // CHUNKS * tile, 2 * depth), jnp.bfloat16),
            pltpu.VMEM((count * tile, 2 * depth), jnp.bfloat16),
            pltpu.VMEM((n, count, tile, tile), jnp.float32),
            pltpu.SemaphoreType.DMA((2,)),
            pltpu.SemaphoreType.DMA((CHUNKS,)),
            pltpu.SemaphoreType.DMA((n,)),
        ],
        compiler_params=pltpu.CompilerParams(vmem_limit_bytes=52 * MIB),
        cost_estimate=pl.CostEstimate(
            flops=4 * n * count * tile * tile * depth, bytes_accessed=6 * MIB, transcendentals=0
        ),
    )(rows, *columns)
    summed = lax.psum_scatter(partial, "z", scatter_dimension=0, tiled=True)[0]
    mirrored = moved(summed, lambda z, y, k: (z, y, z - k))
    arrived = [moved(summed[i], lambda z, y, k, d=OFFSETS[i]: (z, y + d, k)) for i in TURNED]
    updated = pl.pallas_call(
        functools.partial(finish, n, tile, 0.5 / (depth * n)),
        out_shape=jax.ShapeDtypeStruct((n, tile, tile), jnp.float32),
        in_specs=[smem] + [vmem] * (2 + len(TURNED)),
        out_specs=vmem,
        compiler_params=pltpu.CompilerParams(vmem_limit_bytes=16 * MIB),
    )(active.reshape(n), mirrored, *arrived, precision.reshape(n, tile, tile))
    return updated.reshape(precision.shape)


def solution(mesh):
    n = mesh.shape["blk"]
    grid = Mesh(mesh.devices.reshape(n, n, n), AXES)
    rows = ("y", "k")
    in_specs = (P(rows, "z"), P(rows, "z"), P(rows, "z"), P(rows, "z"))
    return jax.shard_map(
        functools.partial(local, n), mesh=grid, in_specs=in_specs, out_specs=P(rows, "z"), check_vma=False
    )
```

```python
import functools

import jax
import jax.numpy as jnp
from jax import lax
from jax.experimental import pallas as pl
from jax.experimental.pallas import tpu as pltpu
from jax.sharding import Mesh, PartitionSpec as P

STEP = 1.0
LASSO = 0.1
RIDGE = 0.5
AXES = ("z", "y", "k")
OFFSETS = (0, 7, 6, 3, 4)
TURNED = (1, 2, 3)
CHUNKS = 2
MIB = 2**20


def join(a_ref, b_ref, out_ref):
    half = a_ref.shape[1]
    out_ref[:, :half] = a_ref[...]
    out_ref[:, half:] = b_ref[...]


def products(n, tile, depth, rows_ref, *refs):
    count = len(OFFSETS)
    columns, (out_ref, rows, picked, made, own_sems, row_sems, out_sems) = refs[:count - 1], refs[count - 1:]
    k = lax.axis_index("k")
    per = n // CHUNKS
    chunks = [
        pltpu.make_async_copy(rows_ref.at[pl.ds(c * per * tile, per * tile)], rows.at[c], row_sems.at[c])
        for c in range(CHUNKS)
    ]
    here = [
        pltpu.make_async_copy(
            rows_ref.at[pl.ds(pl.multiple_of(k * tile, tile), tile), pl.ds((1 - h) * depth, depth)],
            picked.at[pl.ds(0, tile), pl.ds(h * depth, depth)],
            own_sems.at[h],
        )
        for h in range(2)
    ]
    for copy in here + chunks:
        copy.start()
    for i, ref in enumerate(columns, 1):
        picked[i * tile:(i + 1) * tile, :depth] = ref[:, depth:]
        picked[i * tile:(i + 1) * tile, depth:] = ref[:, :depth]
    for copy in here:
        copy.wait()
    stores = []
    for c in range(CHUNKS):
        chunks[c].wait()
        part = lax.dot_general(
            rows[c], picked[...], (((1,), (1,)), ((), ())), preferred_element_type=jnp.float32
        )
        for e in range(per):
            j = c * per + e
            for i in range(count):
                made[j, i] = part[e * tile:(e + 1) * tile, i * tile:(i + 1) * tile]
            m = lax.rem(j + k, n)
            stores.append(pltpu.make_async_copy(made.at[j], out_ref.at[m], out_sems.at[j]))
            stores[-1].start()
    for copy in stores:
        copy.wait()


def finish(n, tile, scale, active_ref, mirrored, *refs):
    arrived, (precision_ref, out_ref) = refs[:-2], refs[-2:]
    z, y, k = (lax.axis_index(a) for a in AXES)
    row = lax.broadcasted_iota(jnp.int32, (tile, tile), 0)
    column = lax.broadcasted_iota(jnp.int32, (tile, tile), 1)

    def put(d, total):
        t = lax.rem(y + d, n)
        w = precision_ref[t]
        gradient = total * scale + RIDGE * w
        if d == 0:
            on_diag = (row == column) & (lax.rem(2 * k - z + n, n) == 0)
            inverse = jnp.where(on_diag, 1.0 / jnp.where(on_diag, w, 1.0), 0.0)
            stepped = w - STEP * (gradient - inverse)
        else:
            stepped = w - STEP * gradient
        shrunk = jnp.where(
            stepped > 0, jnp.maximum(stepped - STEP * LASSO, 0.0), jnp.minimum(stepped + STEP * LASSO, 0.0)
        )
        if d == 0:
            shrunk = jnp.where(on_diag, stepped, shrunk)
        out_ref[t] = shrunk * active_ref[t].astype(jnp.float32)

    for i, d in enumerate(OFFSETS):
        put(d, mirrored[i])
    for i, ref in zip(TURNED, arrived):
        put(n - OFFSETS[i], ref[...].T)


def local(n, resid, samples, precision, active):
    tile, depth = resid.shape
    vmem, smem, far = (pl.BlockSpec(memory_space=s) for s in (pltpu.VMEM, pltpu.SMEM, pltpu.HBM))
    count = len(OFFSETS)

    def moved(a, to):
        def index(z, y, k):
            return (z % n * n + y % n) * n + k % n

        ids = [(z, y, k) for z in range(n) for y in range(n) for k in range(n)]
        return lax.ppermute(a, AXES, [(index(*i), index(*to(*i))) for i in ids])

    own = pl.pallas_call(
        join,
        out_shape=jax.ShapeDtypeStruct((tile, 2 * depth), resid.dtype),
        in_specs=[vmem, vmem],
        out_specs=vmem,
        compiler_params=pltpu.CompilerParams(vmem_limit_bytes=60 * MIB),
    )(resid, samples)
    rows = lax.all_gather(own, "k", axis=0, tiled=True)
    columns = [moved(own, lambda z, y, k, d=d: (z, y - d, k)) for d in OFFSETS[1:]]
    partial = pl.pallas_call(
        functools.partial(products, n, tile, depth),
        out_shape=jax.ShapeDtypeStruct((n, count, tile, tile), jnp.float32),
        in_specs=[far] + [vmem] * (count - 1),
        out_specs=far,
        scratch_shapes=[
            pltpu.VMEM((CHUNKS, n // CHUNKS * tile, 2 * depth), jnp.bfloat16),
            pltpu.VMEM((count * tile, 2 * depth), jnp.bfloat16),
            pltpu.VMEM((n, count, tile, tile), jnp.float32),
            pltpu.SemaphoreType.DMA((2,)),
            pltpu.SemaphoreType.DMA((CHUNKS,)),
            pltpu.SemaphoreType.DMA((n,)),
        ],
        compiler_params=pltpu.CompilerParams(vmem_limit_bytes=52 * MIB),
        cost_estimate=pl.CostEstimate(
            flops=4 * n * count * tile * tile * depth, bytes_accessed=6 * MIB, transcendentals=0
        ),
    )(rows, *columns)
    summed = lax.psum_scatter(partial, "z", scatter_dimension=0, tiled=True)[0]
    mirrored = moved(summed, lambda z, y, k: (z, y, z - k))
    arrived = [moved(summed[i], lambda z, y, k, d=OFFSETS[i]: (z, y + d, k)) for i in TURNED]
    updated = pl.pallas_call(
        functools.partial(finish, n, tile, 0.5 / (depth * n)),
        out_shape=jax.ShapeDtypeStruct((n, tile, tile), jnp.float32),
        in_specs=[smem] + [vmem] * (2 + len(TURNED)),
        out_specs=vmem,
        compiler_params=pltpu.CompilerParams(vmem_limit_bytes=16 * MIB),
    )(active.reshape(n), mirrored, *arrived, precision.reshape(n, tile, tile))
    return updated.reshape(precision.shape)


def solution(mesh):
    n = mesh.shape["blk"]
    grid = Mesh(mesh.devices.reshape(n, n, n), AXES)
    rows = ("y", "k")
    in_specs = (P(rows, "z"), P(rows, "z"), P(rows, "z"), P(rows, "z"))
    return jax.shard_map(
        functools.partial(local, n), mesh=grid, in_specs=in_specs, out_specs=P(rows, "z"), check_vma=False
    )
```

```python
import functools

import jax
import jax.numpy as jnp
from jax import lax
from jax.experimental import pallas as pl
from jax.experimental.pallas import tpu as pltpu
from jax.sharding import Mesh, PartitionSpec as P

STEP = 1.0
LASSO = 0.1
RIDGE = 0.5
AXES = ("z", "y", "k")
EARLY = (0, 7, 6, 4)
TURNED = (1, 2)
LATE = 3
SENT = (7, 6, 3, 4)
CHUNKS = 2
MIB = 2**20


def join(a_ref, b_ref, out_ref):
    half = a_ref.shape[1]
    out_ref[:, :half] = a_ref[...]
    out_ref[:, half:] = b_ref[...]


def products(n, tile, depth, count, offset, rows_ref, *refs):
    columns, (out_ref, rows, picked, made, own_sems, row_sems, out_sems) = refs[:count - offset], refs[count - offset:]
    k = lax.axis_index("k")
    per = n // CHUNKS
    chunks = [
        pltpu.make_async_copy(rows_ref.at[pl.ds(c * per * tile, per * tile)], rows.at[c], row_sems.at[c])
        for c in range(CHUNKS)
    ]
    here = [
        pltpu.make_async_copy(
            rows_ref.at[pl.ds(pl.multiple_of(k * tile, tile), tile), pl.ds((1 - h) * depth, depth)],
            picked.at[pl.ds(0, tile), pl.ds(h * depth, depth)],
            own_sems.at[h],
        )
        for h in range(2 * offset)
    ]
    for copy in here + chunks:
        copy.start()
    for i, ref in enumerate(columns, offset):
        picked[i * tile:(i + 1) * tile, :depth] = ref[:, depth:]
        picked[i * tile:(i + 1) * tile, depth:] = ref[:, :depth]
    for copy in here:
        copy.wait()
    stores = []
    for c in range(CHUNKS):
        chunks[c].wait()
        part = lax.dot_general(
            rows[c], picked[...], (((1,), (1,)), ((), ())), preferred_element_type=jnp.float32
        )
        for e in range(per):
            j = c * per + e
            for i in range(count):
                made[j, i] = part[e * tile:(e + 1) * tile, i * tile:(i + 1) * tile]
            m = lax.rem(j + k, n)
            stores.append(pltpu.make_async_copy(made.at[j], out_ref.at[m], out_sems.at[j]))
            stores[-1].start()
    for copy in stores:
        copy.wait()


def added(parts_ref, out_ref):
    out_ref[...] = jnp.sum(parts_ref[:, 0], axis=0)


def finish(n, tile, scale, active_ref, mirrored, late, *refs):
    arrived, (precision_ref, out_ref) = refs[:-2], refs[-2:]
    z, y, k = (lax.axis_index(a) for a in AXES)
    row = lax.broadcasted_iota(jnp.int32, (tile, tile), 0)
    column = lax.broadcasted_iota(jnp.int32, (tile, tile), 1)

    def put(d, total):
        t = lax.rem(y + d, n)
        w = precision_ref[t]
        gradient = total * scale + RIDGE * w
        if d == 0:
            on_diag = (row == column) & (lax.rem(2 * k - z + n, n) == 0)
            inverse = jnp.where(on_diag, 1.0 / jnp.where(on_diag, w, 1.0), 0.0)
            stepped = w - STEP * (gradient - inverse)
        else:
            stepped = w - STEP * gradient
        shrunk = jnp.where(
            stepped > 0, jnp.maximum(stepped - STEP * LASSO, 0.0), jnp.minimum(stepped + STEP * LASSO, 0.0)
        )
        if d == 0:
            shrunk = jnp.where(on_diag, stepped, shrunk)
        out_ref[t] = shrunk * active_ref[t].astype(jnp.float32)

    put(LATE, late[...])
    for i, d in enumerate(EARLY):
        put(d, mirrored[i])
    for d, ref in zip((LATE,) + tuple(EARLY[i] for i in TURNED), arrived):
        put(n - d, ref[...].T)


def local(n, resid, samples, precision, active):
    tile, depth = resid.shape
    vmem, smem, far = (pl.BlockSpec(memory_space=s) for s in (pltpu.VMEM, pltpu.SMEM, pltpu.HBM))

    def moved(a, to):
        def index(z, y, k):
            return (z % n * n + y % n) * n + k % n

        ids = [(z, y, k) for z in range(n) for y in range(n) for k in range(n)]
        return lax.ppermute(a, AXES, [(index(*i), index(*to(*i))) for i in ids])

    own = pl.pallas_call(
        join,
        out_shape=jax.ShapeDtypeStruct((tile, 2 * depth), resid.dtype),
        in_specs=[vmem, vmem],
        out_specs=vmem,
        compiler_params=pltpu.CompilerParams(vmem_limit_bytes=60 * MIB),
    )(resid, samples)
    rows = lax.all_gather(own, "k", axis=0, tiled=True)
    panel = {d: moved(own, lambda z, y, k, d=d: (z, y - d, k)) for d in SENT}

    def multiplied(columns, offset, flops):
        count = len(columns) + offset
        return pl.pallas_call(
            functools.partial(products, n, tile, depth, count, offset),
            out_shape=jax.ShapeDtypeStruct((n, count, tile, tile), jnp.float32),
            in_specs=[far] + [vmem] * len(columns),
            out_specs=far,
            scratch_shapes=[
                pltpu.VMEM((CHUNKS, n // CHUNKS * tile, 2 * depth), jnp.bfloat16),
                pltpu.VMEM((count * tile, 2 * depth), jnp.bfloat16),
                pltpu.VMEM((n, count, tile, tile), jnp.float32),
                pltpu.SemaphoreType.DMA((2,)),
                pltpu.SemaphoreType.DMA((CHUNKS,)),
                pltpu.SemaphoreType.DMA((n,)),
            ],
            compiler_params=pltpu.CompilerParams(vmem_limit_bytes=52 * MIB),
            cost_estimate=pl.CostEstimate(flops=flops, bytes_accessed=6 * MIB, transcendentals=0),
        )(rows, *columns)

    once = 4 * n * tile * tile * depth
    early = lax.psum_scatter(
        multiplied([panel[d] for d in EARLY[1:]], 1, once), "z", scatter_dimension=0, tiled=True
    )[0]
    weight = 600 * once
    parts = lax.all_to_all(multiplied([panel[LATE]], 0, weight), "z", 0, 0, tiled=True)
    late = pl.pallas_call(
        added,
        out_shape=jax.ShapeDtypeStruct((tile, tile), jnp.float32),
        in_specs=[vmem],
        out_specs=vmem,
        compiler_params=pltpu.CompilerParams(vmem_limit_bytes=16 * MIB),
    )(parts)
    arrived = [moved(late, lambda z, y, k: (z, y + LATE, k))]
    late = moved(late, lambda z, y, k: (z, y, z - k))
    mirrored = moved(early, lambda z, y, k: (z, y, z - k))
    arrived += [moved(early[i], lambda z, y, k, d=EARLY[i]: (z, y + d, k)) for i in TURNED]
    updated = pl.pallas_call(
        functools.partial(finish, n, tile, 0.5 / (depth * n)),
        out_shape=jax.ShapeDtypeStruct((n, tile, tile), jnp.float32),
        in_specs=[smem] + [vmem] * (3 + len(arrived)),
        out_specs=vmem,
        compiler_params=pltpu.CompilerParams(vmem_limit_bytes=16 * MIB),
    )(active.reshape(n), mirrored, late, *arrived, precision.reshape(n, tile, tile))
    return updated.reshape(precision.shape)


def solution(mesh):
    n = mesh.shape["blk"]
    grid = Mesh(mesh.devices.reshape(n, n, n), AXES)
    rows = ("y", "k")
    in_specs = (P(rows, "z"), P(rows, "z"), P(rows, "z"), P(rows, "z"))
    return jax.shard_map(
        functools.partial(local, n), mesh=grid, in_specs=in_specs, out_specs=P(rows, "z"), check_vma=False
    )
```

```python
import functools

import jax
import jax.numpy as jnp
from jax import lax
from jax.experimental import pallas as pl
from jax.experimental.pallas import tpu as pltpu
from jax.sharding import Mesh, PartitionSpec as P

STEP = 1.0
LASSO = 0.1
RIDGE = 0.5
AXES = ("z", "y", "k")
EARLY = (0, 7, 2, 4)
TURNED = (1, 2)
LATE = 5
SENT = (7, 2, 5, 4)
CHUNKS = 2
MIB = 2**20


def join(a_ref, b_ref, out_ref):
    half = a_ref.shape[1]
    out_ref[:, :half] = a_ref[...]
    out_ref[:, half:] = b_ref[...]


def products(n, tile, depth, count, offset, rows_ref, *refs):
    columns, (out_ref, rows, picked, made, own_sems, row_sems, out_sems) = refs[:count - offset], refs[count - offset:]
    k = lax.axis_index("k")
    per = n // CHUNKS
    chunks = [
        pltpu.make_async_copy(rows_ref.at[pl.ds(c * per * tile, per * tile)], rows.at[c], row_sems.at[c])
        for c in range(CHUNKS)
    ]
    here = [
        pltpu.make_async_copy(
            rows_ref.at[pl.ds(pl.multiple_of(k * tile, tile), tile), pl.ds((1 - h) * depth, depth)],
            picked.at[pl.ds(0, tile), pl.ds(h * depth, depth)],
            own_sems.at[h],
        )
        for h in range(2 * offset)
    ]
    for copy in here + chunks:
        copy.start()
    for i, ref in enumerate(columns, offset):
        picked[i * tile:(i + 1) * tile, :depth] = ref[:, depth:]
        picked[i * tile:(i + 1) * tile, depth:] = ref[:, :depth]
    for copy in here:
        copy.wait()
    stores = []
    for c in range(CHUNKS):
        chunks[c].wait()
        part = lax.dot_general(
            rows[c], picked[...], (((1,), (1,)), ((), ())), preferred_element_type=jnp.float32
        )
        for e in range(per):
            j = c * per + e
            for i in range(count):
                made[j, i] = part[e * tile:(e + 1) * tile, i * tile:(i + 1) * tile]
            m = lax.rem(j + k, n)
            stores.append(pltpu.make_async_copy(made.at[j], out_ref.at[m], out_sems.at[j]))
            stores[-1].start()
    for copy in stores:
        copy.wait()


def added(parts_ref, out_ref):
    out_ref[...] = jnp.sum(parts_ref[:, 0], axis=0)


def finish(n, tile, scale, active_ref, mirrored, late, *refs):
    arrived, (precision_ref, out_ref) = refs[:-2], refs[-2:]
    z, y, k = (lax.axis_index(a) for a in AXES)
    row = lax.broadcasted_iota(jnp.int32, (tile, tile), 0)
    column = lax.broadcasted_iota(jnp.int32, (tile, tile), 1)

    def put(d, total):
        t = lax.rem(y + d, n)
        w = precision_ref[t]
        gradient = total * scale + RIDGE * w
        if d == 0:
            on_diag = (row == column) & (lax.rem(2 * k - z + n, n) == 0)
            inverse = jnp.where(on_diag, 1.0 / jnp.where(on_diag, w, 1.0), 0.0)
            stepped = w - STEP * (gradient - inverse)
        else:
            stepped = w - STEP * gradient
        shrunk = jnp.where(
            stepped > 0, jnp.maximum(stepped - STEP * LASSO, 0.0), jnp.minimum(stepped + STEP * LASSO, 0.0)
        )
        if d == 0:
            shrunk = jnp.where(on_diag, stepped, shrunk)
        out_ref[t] = shrunk * active_ref[t].astype(jnp.float32)

    put(LATE, late[...])
    for i, d in enumerate(EARLY):
        put(d, mirrored[i])
    for d, ref in zip((LATE,) + tuple(EARLY[i] for i in TURNED), arrived):
        put(n - d, ref[...].T)


def local(n, resid, samples, precision, active):
    tile, depth = resid.shape
    vmem, smem, far = (pl.BlockSpec(memory_space=s) for s in (pltpu.VMEM, pltpu.SMEM, pltpu.HBM))

    def moved(a, to):
        def index(z, y, k):
            return (z % n * n + y % n) * n + k % n

        ids = [(z, y, k) for z in range(n) for y in range(n) for k in range(n)]
        return lax.ppermute(a, AXES, [(index(*i), index(*to(*i))) for i in ids])

    own = pl.pallas_call(
        join,
        out_shape=jax.ShapeDtypeStruct((tile, 2 * depth), resid.dtype),
        in_specs=[vmem, vmem],
        out_specs=vmem,
        compiler_params=pltpu.CompilerParams(vmem_limit_bytes=60 * MIB),
    )(resid, samples)
    rows = lax.all_gather(own, "k", axis=0, tiled=True)
    panel = {d: moved(own, lambda z, y, k, d=d: (z, y - d, k)) for d in SENT}

    def multiplied(columns, offset, flops):
        count = len(columns) + offset
        return pl.pallas_call(
            functools.partial(products, n, tile, depth, count, offset),
            out_shape=jax.ShapeDtypeStruct((n, count, tile, tile), jnp.float32),
            in_specs=[far] + [vmem] * len(columns),
            out_specs=far,
            scratch_shapes=[
                pltpu.VMEM((CHUNKS, n // CHUNKS * tile, 2 * depth), jnp.bfloat16),
                pltpu.VMEM((count * tile, 2 * depth), jnp.bfloat16),
                pltpu.VMEM((n, count, tile, tile), jnp.float32),
                pltpu.SemaphoreType.DMA((2,)),
                pltpu.SemaphoreType.DMA((CHUNKS,)),
                pltpu.SemaphoreType.DMA((n,)),
            ],
            compiler_params=pltpu.CompilerParams(vmem_limit_bytes=52 * MIB),
            cost_estimate=pl.CostEstimate(flops=flops, bytes_accessed=6 * MIB, transcendentals=0),
        )(rows, *columns)

    once = 4 * n * tile * tile * depth
    early = lax.psum_scatter(
        multiplied([panel[d] for d in EARLY[1:]], 1, once), "z", scatter_dimension=0, tiled=True
    )[0]
    weight = 600 * once
    parts = lax.all_to_all(multiplied([panel[LATE]], 0, weight), "z", 0, 0, tiled=True)
    late = pl.pallas_call(
        added,
        out_shape=jax.ShapeDtypeStruct((tile, tile), jnp.float32),
        in_specs=[vmem],
        out_specs=vmem,
        compiler_params=pltpu.CompilerParams(vmem_limit_bytes=16 * MIB),
    )(parts)
    arrived = [moved(late, lambda z, y, k: (z, y + LATE, k))]
    late = moved(late, lambda z, y, k: (z, y, z - k))
    mirrored = moved(early, lambda z, y, k: (z, y, z - k))
    arrived += [moved(early[i], lambda z, y, k, d=EARLY[i]: (z, y + d, k)) for i in TURNED]
    updated = pl.pallas_call(
        functools.partial(finish, n, tile, 0.5 / (depth * n)),
        out_shape=jax.ShapeDtypeStruct((n, tile, tile), jnp.float32),
        in_specs=[smem] + [vmem] * (3 + len(arrived)),
        out_specs=vmem,
        compiler_params=pltpu.CompilerParams(vmem_limit_bytes=16 * MIB),
    )(active.reshape(n), mirrored, late, *arrived, precision.reshape(n, tile, tile))
    return updated.reshape(precision.shape)


def solution(mesh):
    n = mesh.shape["blk"]
    grid = Mesh(mesh.devices.reshape(n, n, n), AXES)
    rows = ("y", "k")
    in_specs = (P(rows, "z"), P(rows, "z"), P(rows, "z"), P(rows, "z"))
    return jax.shard_map(
        functools.partial(local, n), mesh=grid, in_specs=in_specs, out_specs=P(rows, "z"), check_vma=False
    )
```

```python
import functools

import jax
import jax.numpy as jnp
from jax import lax
from jax.experimental import pallas as pl
from jax.experimental.pallas import tpu as pltpu
from jax.sharding import Mesh, PartitionSpec as P

STEP = 1.0
LASSO = 0.1
RIDGE = 0.5
AXES = ("z", "y", "k")
EARLY = (0, 7, 6, 4)
TURNED = (1, 2)
LATE = 3
SENT = (7, 6, 3, 4)
CHUNKS = 2
MIB = 2**20


def join(a_ref, b_ref, out_ref):
    half = a_ref.shape[1]
    out_ref[:, :half] = a_ref[...]
    out_ref[:, half:] = b_ref[...]


def products(n, tile, depth, count, offset, resid_ref, samples_ref, *refs):
    columns, (out_ref, rows, picked, made, own_sems, row_sems, out_sems) = refs[:count - offset], refs[count - offset:]
    k = lax.axis_index("k")
    per = n // CHUNKS
    halves = resid_ref, samples_ref
    chunks = [
        pltpu.make_async_copy(
            halves[h].at[pl.ds(c * per * tile, per * tile)],
            rows.at[c, :, pl.ds(h * depth, depth)],
            row_sems.at[c, h],
        )
        for c in range(CHUNKS)
        for h in range(2)
    ]
    here = [
        pltpu.make_async_copy(
            halves[1 - h].at[pl.ds(pl.multiple_of(k * tile, tile), tile)],
            picked.at[pl.ds(0, tile), pl.ds(h * depth, depth)],
            own_sems.at[h],
        )
        for h in range(2 * offset)
    ]
    for copy in here + chunks:
        copy.start()
    for i, ref in enumerate(columns, offset):
        picked[i * tile:(i + 1) * tile, :depth] = ref[:, depth:]
        picked[i * tile:(i + 1) * tile, depth:] = ref[:, :depth]
    for copy in here:
        copy.wait()
    stores = []
    for c in range(CHUNKS):
        for h in range(2):
            chunks[2 * c + h].wait()
        part = lax.dot_general(
            rows[c], picked[...], (((1,), (1,)), ((), ())), preferred_element_type=jnp.float32
        )
        for e in range(per):
            j = c * per + e
            for i in range(count):
                made[j, i] = part[e * tile:(e + 1) * tile, i * tile:(i + 1) * tile]
            m = lax.rem(j + k, n)
            stores.append(pltpu.make_async_copy(made.at[j], out_ref.at[m], out_sems.at[j]))
            stores[-1].start()
    for copy in stores:
        copy.wait()


def added(parts_ref, out_ref):
    out_ref[...] = jnp.sum(parts_ref[:, 0], axis=0)


def finish(n, tile, scale, active_ref, mirrored, late, *refs):
    arrived, (precision_ref, out_ref) = refs[:-2], refs[-2:]
    z, y, k = (lax.axis_index(a) for a in AXES)
    row = lax.broadcasted_iota(jnp.int32, (tile, tile), 0)
    column = lax.broadcasted_iota(jnp.int32, (tile, tile), 1)

    def put(d, total):
        t = lax.rem(y + d, n)
        w = precision_ref[t]
        gradient = total * scale + RIDGE * w
        if d == 0:
            on_diag = (row == column) & (lax.rem(2 * k - z + n, n) == 0)
            inverse = jnp.where(on_diag, 1.0 / jnp.where(on_diag, w, 1.0), 0.0)
            stepped = w - STEP * (gradient - inverse)
        else:
            stepped = w - STEP * gradient
        shrunk = jnp.where(
            stepped > 0, jnp.maximum(stepped - STEP * LASSO, 0.0), jnp.minimum(stepped + STEP * LASSO, 0.0)
        )
        if d == 0:
            shrunk = jnp.where(on_diag, stepped, shrunk)
        out_ref[t] = shrunk * active_ref[t].astype(jnp.float32)

    put(LATE, late[...])
    for i, d in enumerate(EARLY):
        put(d, mirrored[i])
    for d, ref in zip((LATE,) + tuple(EARLY[i] for i in TURNED), arrived):
        put(n - d, ref[...].T)


def local(n, resid, samples, precision, active):
    tile, depth = resid.shape
    vmem, smem, far = (pl.BlockSpec(memory_space=s) for s in (pltpu.VMEM, pltpu.SMEM, pltpu.HBM))

    def moved(a, to):
        def index(z, y, k):
            return (z % n * n + y % n) * n + k % n

        ids = [(z, y, k) for z in range(n) for y in range(n) for k in range(n)]
        return lax.ppermute(a, AXES, [(index(*i), index(*to(*i))) for i in ids])

    own = pl.pallas_call(
        join,
        out_shape=jax.ShapeDtypeStruct((tile, 2 * depth), resid.dtype),
        in_specs=[vmem, vmem],
        out_specs=vmem,
        compiler_params=pltpu.CompilerParams(vmem_limit_bytes=60 * MIB),
    )(resid, samples)
    halves = lax.all_gather((resid, samples), "k", axis=0, tiled=True)
    panel = {d: moved(own, lambda z, y, k, d=d: (z, y - d, k)) for d in SENT}

    def multiplied(columns, offset, flops):
        count = len(columns) + offset
        return pl.pallas_call(
            functools.partial(products, n, tile, depth, count, offset),
            out_shape=jax.ShapeDtypeStruct((n, count, tile, tile), jnp.float32),
            in_specs=[far, far] + [vmem] * len(columns),
            out_specs=far,
            scratch_shapes=[
                pltpu.VMEM((CHUNKS, n // CHUNKS * tile, 2 * depth), jnp.bfloat16),
                pltpu.VMEM((count * tile, 2 * depth), jnp.bfloat16),
                pltpu.VMEM((n, count, tile, tile), jnp.float32),
                pltpu.SemaphoreType.DMA((2,)),
                pltpu.SemaphoreType.DMA((CHUNKS, 2)),
                pltpu.SemaphoreType.DMA((n,)),
            ],
            compiler_params=pltpu.CompilerParams(vmem_limit_bytes=52 * MIB),
            cost_estimate=pl.CostEstimate(flops=flops, bytes_accessed=6 * MIB, transcendentals=0),
        )(*halves, *columns)

    once = 4 * n * tile * tile * depth
    early = lax.psum_scatter(
        multiplied([panel[d] for d in EARLY[1:]], 1, once), "z", scatter_dimension=0, tiled=True
    )[0]
    weight = 600 * once
    parts = lax.all_to_all(multiplied([panel[LATE]], 0, weight), "z", 0, 0, tiled=True)
    late = pl.pallas_call(
        added,
        out_shape=jax.ShapeDtypeStruct((tile, tile), jnp.float32),
        in_specs=[vmem],
        out_specs=vmem,
        compiler_params=pltpu.CompilerParams(vmem_limit_bytes=16 * MIB),
    )(parts)
    arrived = [moved(late, lambda z, y, k: (z, y + LATE, k))]
    late = moved(late, lambda z, y, k: (z, y, z - k))
    mirrored = moved(early, lambda z, y, k: (z, y, z - k))
    arrived += [moved(early[i], lambda z, y, k, d=EARLY[i]: (z, y + d, k)) for i in TURNED]
    updated = pl.pallas_call(
        functools.partial(finish, n, tile, 0.5 / (depth * n)),
        out_shape=jax.ShapeDtypeStruct((n, tile, tile), jnp.float32),
        in_specs=[smem] + [vmem] * (3 + len(arrived)),
        out_specs=vmem,
        compiler_params=pltpu.CompilerParams(vmem_limit_bytes=16 * MIB),
    )(active.reshape(n), mirrored, late, *arrived, precision.reshape(n, tile, tile))
    return updated.reshape(precision.shape)


def solution(mesh):
    n = mesh.shape["blk"]
    grid = Mesh(mesh.devices.reshape(n, n, n), AXES)
    rows = ("y", "k")
    in_specs = (P(rows, "z"), P(rows, "z"), P(rows, "z"), P(rows, "z"))
    return jax.shard_map(
        functools.partial(local, n), mesh=grid, in_specs=in_specs, out_specs=P(rows, "z"), check_vma=False
    )
```

```python
import functools

import jax
import jax.numpy as jnp
from jax import lax
from jax.experimental import pallas as pl
from jax.experimental.pallas import tpu as pltpu
from jax.sharding import Mesh, PartitionSpec as P

STEP = 1.0
LASSO = 0.1
RIDGE = 0.5
AXES = ("z", "y", "k")
EARLY = (0, 7, 4)
TURNED = (1,)
LATE = (3, 6)
SENT = (7, 4, 3, 6)
CHUNKS = 2
MIB = 2**20


def join(a_ref, b_ref, out_ref):
    half = a_ref.shape[1]
    out_ref[:, :half] = a_ref[...]
    out_ref[:, half:] = b_ref[...]


def products(n, tile, depth, count, offset, rows_ref, *refs):
    columns, (out_ref, rows, picked, made, own_sems, row_sems, out_sems) = refs[:count - offset], refs[count - offset:]
    k = lax.axis_index("k")
    per = n // CHUNKS
    chunks = [
        pltpu.make_async_copy(rows_ref.at[pl.ds(c * per * tile, per * tile)], rows.at[c], row_sems.at[c])
        for c in range(CHUNKS)
    ]
    here = [
        pltpu.make_async_copy(
            rows_ref.at[pl.ds(pl.multiple_of(k * tile, tile), tile), pl.ds((1 - h) * depth, depth)],
            picked.at[pl.ds(0, tile), pl.ds(h * depth, depth)],
            own_sems.at[h],
        )
        for h in range(2 * offset)
    ]
    for copy in here + chunks:
        copy.start()
    for i, ref in enumerate(columns, offset):
        picked[i * tile:(i + 1) * tile, :depth] = ref[:, depth:]
        picked[i * tile:(i + 1) * tile, depth:] = ref[:, :depth]
    for copy in here:
        copy.wait()
    stores = []
    for c in range(CHUNKS):
        chunks[c].wait()
        part = lax.dot_general(
            rows[c], picked[...], (((1,), (1,)), ((), ())), preferred_element_type=jnp.float32
        )
        for e in range(per):
            j = c * per + e
            for i in range(count):
                made[j, i] = part[e * tile:(e + 1) * tile, i * tile:(i + 1) * tile]
            m = lax.rem(j + k, n)
            stores.append(pltpu.make_async_copy(made.at[j], out_ref.at[m], out_sems.at[j]))
            stores[-1].start()
    for copy in stores:
        copy.wait()


def added(parts_ref, out_ref, *each):
    for i, ref in enumerate(each):
        total = jnp.sum(parts_ref[:, i], axis=0)
        out_ref[i] = total
        ref[...] = total


def finish(n, tile, scale, active_ref, mirrored, late, *refs):
    arrived, (precision_ref, out_ref) = refs[:-2], refs[-2:]
    z, y, k = (lax.axis_index(a) for a in AXES)
    row = lax.broadcasted_iota(jnp.int32, (tile, tile), 0)
    column = lax.broadcasted_iota(jnp.int32, (tile, tile), 1)

    def put(d, total):
        t = lax.rem(y + d, n)
        w = precision_ref[t]
        gradient = total * scale + RIDGE * w
        if d == 0:
            on_diag = (row == column) & (lax.rem(2 * k - z + n, n) == 0)
            inverse = jnp.where(on_diag, 1.0 / jnp.where(on_diag, w, 1.0), 0.0)
            stepped = w - STEP * (gradient - inverse)
        else:
            stepped = w - STEP * gradient
        shrunk = jnp.where(
            stepped > 0, jnp.maximum(stepped - STEP * LASSO, 0.0), jnp.minimum(stepped + STEP * LASSO, 0.0)
        )
        if d == 0:
            shrunk = jnp.where(on_diag, stepped, shrunk)
        out_ref[t] = shrunk * active_ref[t].astype(jnp.float32)

    for i, d in enumerate(LATE):
        put(d, late[i])
    for i, d in enumerate(EARLY):
        put(d, mirrored[i])
    for d, ref in zip(LATE + tuple(EARLY[i] for i in TURNED), arrived):
        put(n - d, ref[...].T)


def local(n, resid, samples, precision, active):
    tile, depth = resid.shape
    vmem, smem, far = (pl.BlockSpec(memory_space=s) for s in (pltpu.VMEM, pltpu.SMEM, pltpu.HBM))

    def moved(a, to):
        def index(z, y, k):
            return (z % n * n + y % n) * n + k % n

        ids = [(z, y, k) for z in range(n) for y in range(n) for k in range(n)]
        return lax.ppermute(a, AXES, [(index(*i), index(*to(*i))) for i in ids])

    own = pl.pallas_call(
        join,
        out_shape=jax.ShapeDtypeStruct((tile, 2 * depth), resid.dtype),
        in_specs=[vmem, vmem],
        out_specs=vmem,
        compiler_params=pltpu.CompilerParams(vmem_limit_bytes=60 * MIB),
    )(resid, samples)
    rows = lax.all_gather(own, "k", axis=0, tiled=True)
    panel = {d: moved(own, lambda z, y, k, d=d: (z, y - d, k)) for d in SENT}

    def multiplied(columns, offset, flops):
        count = len(columns) + offset
        return pl.pallas_call(
            functools.partial(products, n, tile, depth, count, offset),
            out_shape=jax.ShapeDtypeStruct((n, count, tile, tile), jnp.float32),
            in_specs=[far] + [vmem] * len(columns),
            out_specs=far,
            scratch_shapes=[
                pltpu.VMEM((CHUNKS, n // CHUNKS * tile, 2 * depth), jnp.bfloat16),
                pltpu.VMEM((count * tile, 2 * depth), jnp.bfloat16),
                pltpu.VMEM((n, count, tile, tile), jnp.float32),
                pltpu.SemaphoreType.DMA((2,)),
                pltpu.SemaphoreType.DMA((CHUNKS,)),
                pltpu.SemaphoreType.DMA((n,)),
            ],
            compiler_params=pltpu.CompilerParams(vmem_limit_bytes=52 * MIB),
            cost_estimate=pl.CostEstimate(flops=flops, bytes_accessed=6 * MIB, transcendentals=0),
        )(rows, *columns)

    once = 4 * n * tile * tile * depth
    early = lax.psum_scatter(
        multiplied([panel[d] for d in EARLY[1:]], 1, once), "z", scatter_dimension=0, tiled=True
    )[0]
    weight = 600 * once
    parts = lax.all_to_all(multiplied([panel[d] for d in LATE], 0, weight), "z", 0, 0, tiled=True)
    square = jax.ShapeDtypeStruct((tile, tile), jnp.float32)
    late, *each = pl.pallas_call(
        added,
        out_shape=[jax.ShapeDtypeStruct((len(LATE), tile, tile), jnp.float32)] + [square] * len(LATE),
        in_specs=[vmem],
        out_specs=[vmem] * (1 + len(LATE)),
        compiler_params=pltpu.CompilerParams(vmem_limit_bytes=16 * MIB),
    )(parts)
    arrived = [moved(a, lambda z, y, k, d=d: (z, y + d, k)) for a, d in zip(each, LATE)]
    late = moved(late, lambda z, y, k: (z, y, z - k))
    mirrored = moved(early, lambda z, y, k: (z, y, z - k))
    arrived += [moved(early[i], lambda z, y, k, d=EARLY[i]: (z, y + d, k)) for i in TURNED]
    updated = pl.pallas_call(
        functools.partial(finish, n, tile, 0.5 / (depth * n)),
        out_shape=jax.ShapeDtypeStruct((n, tile, tile), jnp.float32),
        in_specs=[smem] + [vmem] * (3 + len(arrived)),
        out_specs=vmem,
        compiler_params=pltpu.CompilerParams(vmem_limit_bytes=16 * MIB),
    )(active.reshape(n), mirrored, late, *arrived, precision.reshape(n, tile, tile))
    return updated.reshape(precision.shape)


def solution(mesh):
    n = mesh.shape["blk"]
    grid = Mesh(mesh.devices.reshape(n, n, n), AXES)
    rows = ("y", "k")
    in_specs = (P(rows, "z"), P(rows, "z"), P(rows, "z"), P(rows, "z"))
    return jax.shard_map(
        functools.partial(local, n), mesh=grid, in_specs=in_specs, out_specs=P(rows, "z"), check_vma=False
    )
```

```python
import functools

import jax
import jax.numpy as jnp
from jax import lax
from jax.experimental import pallas as pl
from jax.experimental.pallas import tpu as pltpu
from jax.sharding import Mesh, PartitionSpec as P

STEP = 1.0
LASSO = 0.1
RIDGE = 0.5
AXES = ("z", "y", "k")
EARLY = (0, 7, 1, 6, 4)
TURNED = (3,)
LATE = 3
SENT = (7, 1, 6, 3, 4)
CHUNKS = 2
MIB = 2**20


def join(a_ref, b_ref, out_ref):
    half = a_ref.shape[1]
    out_ref[:, :half] = a_ref[...]
    out_ref[:, half:] = b_ref[...]


def products(n, tile, depth, count, offset, rows_ref, *refs):
    columns, (out_ref, rows, picked, made, own_sems, row_sems, out_sems) = refs[:count - offset], refs[count - offset:]
    k = lax.axis_index("k")
    per = n // CHUNKS
    chunks = [
        pltpu.make_async_copy(rows_ref.at[pl.ds(c * per * tile, per * tile)], rows.at[c], row_sems.at[c])
        for c in range(CHUNKS)
    ]
    here = [
        pltpu.make_async_copy(
            rows_ref.at[pl.ds(pl.multiple_of(k * tile, tile), tile), pl.ds((1 - h) * depth, depth)],
            picked.at[pl.ds(0, tile), pl.ds(h * depth, depth)],
            own_sems.at[h],
        )
        for h in range(2 * offset)
    ]
    for copy in here + chunks:
        copy.start()
    for i, ref in enumerate(columns, offset):
        picked[i * tile:(i + 1) * tile, :depth] = ref[:, depth:]
        picked[i * tile:(i + 1) * tile, depth:] = ref[:, :depth]
    for copy in here:
        copy.wait()
    stores = []
    for c in range(CHUNKS):
        chunks[c].wait()
        part = lax.dot_general(
            rows[c], picked[...], (((1,), (1,)), ((), ())), preferred_element_type=jnp.float32
        )
        for e in range(per):
            j = c * per + e
            for i in range(count):
                made[j, i] = part[e * tile:(e + 1) * tile, i * tile:(i + 1) * tile]
            m = lax.rem(j + k, n)
            stores.append(pltpu.make_async_copy(made.at[j], out_ref.at[m], out_sems.at[j]))
            stores[-1].start()
    for copy in stores:
        copy.wait()


def added(parts_ref, out_ref):
    out_ref[...] = jnp.sum(parts_ref[:, 0], axis=0)


def finish(n, tile, scale, active_ref, mirrored, late, *refs):
    arrived, (precision_ref, out_ref) = refs[:-2], refs[-2:]
    z, y, k = (lax.axis_index(a) for a in AXES)
    row = lax.broadcasted_iota(jnp.int32, (tile, tile), 0)
    column = lax.broadcasted_iota(jnp.int32, (tile, tile), 1)

    def put(d, total):
        t = lax.rem(y + d, n)
        w = precision_ref[t]
        gradient = total * scale + RIDGE * w
        if d == 0:
            on_diag = (row == column) & (lax.rem(2 * k - z + n, n) == 0)
            inverse = jnp.where(on_diag, 1.0 / jnp.where(on_diag, w, 1.0), 0.0)
            stepped = w - STEP * (gradient - inverse)
        else:
            stepped = w - STEP * gradient
        shrunk = jnp.where(
            stepped > 0, jnp.maximum(stepped - STEP * LASSO, 0.0), jnp.minimum(stepped + STEP * LASSO, 0.0)
        )
        if d == 0:
            shrunk = jnp.where(on_diag, stepped, shrunk)
        out_ref[t] = shrunk * active_ref[t].astype(jnp.float32)

    put(LATE, late[...])
    for i, d in enumerate(EARLY):
        put(d, mirrored[i])
    for d, ref in zip((LATE,) + tuple(EARLY[i] for i in TURNED), arrived):
        put(n - d, ref[...].T)


def local(n, resid, samples, precision, active):
    tile, depth = resid.shape
    vmem, smem, far = (pl.BlockSpec(memory_space=s) for s in (pltpu.VMEM, pltpu.SMEM, pltpu.HBM))

    def moved(a, to):
        def index(z, y, k):
            return (z % n * n + y % n) * n + k % n

        ids = [(z, y, k) for z in range(n) for y in range(n) for k in range(n)]
        return lax.ppermute(a, AXES, [(index(*i), index(*to(*i))) for i in ids])

    own = pl.pallas_call(
        join,
        out_shape=jax.ShapeDtypeStruct((tile, 2 * depth), resid.dtype),
        in_specs=[vmem, vmem],
        out_specs=vmem,
        compiler_params=pltpu.CompilerParams(vmem_limit_bytes=60 * MIB),
    )(resid, samples)
    rows = lax.all_gather(own, "k", axis=0, tiled=True)
    panel = {d: moved(own, lambda z, y, k, d=d: (z, y - d, k)) for d in SENT}

    def multiplied(columns, offset, flops):
        count = len(columns) + offset
        return pl.pallas_call(
            functools.partial(products, n, tile, depth, count, offset),
            out_shape=jax.ShapeDtypeStruct((n, count, tile, tile), jnp.float32),
            in_specs=[far] + [vmem] * len(columns),
            out_specs=far,
            scratch_shapes=[
                pltpu.VMEM((CHUNKS, n // CHUNKS * tile, 2 * depth), jnp.bfloat16),
                pltpu.VMEM((count * tile, 2 * depth), jnp.bfloat16),
                pltpu.VMEM((n, count, tile, tile), jnp.float32),
                pltpu.SemaphoreType.DMA((2,)),
                pltpu.SemaphoreType.DMA((CHUNKS,)),
                pltpu.SemaphoreType.DMA((n,)),
            ],
            compiler_params=pltpu.CompilerParams(vmem_limit_bytes=52 * MIB),
            cost_estimate=pl.CostEstimate(flops=flops, bytes_accessed=6 * MIB, transcendentals=0),
        )(rows, *columns)

    once = 4 * n * tile * tile * depth
    early = lax.psum_scatter(
        multiplied([panel[d] for d in EARLY[1:]], 1, once), "z", scatter_dimension=0, tiled=True
    )[0]
    weight = 600 * once
    parts = lax.all_to_all(multiplied([panel[LATE]], 0, weight), "z", 0, 0, tiled=True)
    late = pl.pallas_call(
        added,
        out_shape=jax.ShapeDtypeStruct((tile, tile), jnp.float32),
        in_specs=[vmem],
        out_specs=vmem,
        compiler_params=pltpu.CompilerParams(vmem_limit_bytes=16 * MIB),
    )(parts)
    arrived = [moved(late, lambda z, y, k: (z, y + LATE, k))]
    late = moved(late, lambda z, y, k: (z, y, z - k))
    mirrored = moved(early, lambda z, y, k: (z, y, z - k))
    arrived += [moved(early[i], lambda z, y, k, d=EARLY[i]: (z, y + d, k)) for i in TURNED]
    updated = pl.pallas_call(
        functools.partial(finish, n, tile, 0.5 / (depth * n)),
        out_shape=jax.ShapeDtypeStruct((n, tile, tile), jnp.float32),
        in_specs=[smem] + [vmem] * (3 + len(arrived)),
        out_specs=vmem,
        compiler_params=pltpu.CompilerParams(vmem_limit_bytes=16 * MIB),
    )(active.reshape(n), mirrored, late, *arrived, precision.reshape(n, tile, tile))
    return updated.reshape(precision.shape)


def solution(mesh):
    n = mesh.shape["blk"]
    grid = Mesh(mesh.devices.reshape(n, n, n), AXES)
    rows = ("y", "k")
    in_specs = (P(rows, "z"), P(rows, "z"), P(rows, "z"), P(rows, "z"))
    return jax.shard_map(
        functools.partial(local, n), mesh=grid, in_specs=in_specs, out_specs=P(rows, "z"), check_vma=False
    )
```

```python
import functools

import jax
import jax.numpy as jnp
from jax import lax
from jax.experimental import pallas as pl
from jax.experimental.pallas import tpu as pltpu
from jax.sharding import Mesh, PartitionSpec as P

STEP = 1.0
LASSO = 0.1
RIDGE = 0.5
AXES = ("z", "y", "k")
EARLY = (0, 1, 2, 4)
TURNED = (1, 2)
LATE = 5
SENT = (1, 2, 5, 4)
CHUNKS = 2
MIB = 2**20


def join(a_ref, b_ref, out_ref):
    half = a_ref.shape[1]
    out_ref[:, :half] = a_ref[...]
    out_ref[:, half:] = b_ref[...]


def products(n, tile, depth, count, offset, rows_ref, *refs):
    columns, (out_ref, rows, picked, made, own_sems, row_sems, out_sems) = refs[:count - offset], refs[count - offset:]
    k = lax.axis_index("k")
    per = n // CHUNKS
    chunks = [
        pltpu.make_async_copy(rows_ref.at[pl.ds(c * per * tile, per * tile)], rows.at[c], row_sems.at[c])
        for c in range(CHUNKS)
    ]
    here = [
        pltpu.make_async_copy(
            rows_ref.at[pl.ds(pl.multiple_of(k * tile, tile), tile), pl.ds((1 - h) * depth, depth)],
            picked.at[pl.ds(0, tile), pl.ds(h * depth, depth)],
            own_sems.at[h],
        )
        for h in range(2 * offset)
    ]
    for copy in here + chunks:
        copy.start()
    for i, ref in enumerate(columns, offset):
        picked[i * tile:(i + 1) * tile, :depth] = ref[:, depth:]
        picked[i * tile:(i + 1) * tile, depth:] = ref[:, :depth]
    for copy in here:
        copy.wait()
    stores = []
    for c in range(CHUNKS):
        chunks[c].wait()
        part = lax.dot_general(
            rows[c], picked[...], (((1,), (1,)), ((), ())), preferred_element_type=jnp.float32
        )
        for e in range(per):
            j = c * per + e
            for i in range(count):
                made[j, i] = part[e * tile:(e + 1) * tile, i * tile:(i + 1) * tile]
            m = lax.rem(j + k, n)
            stores.append(pltpu.make_async_copy(made.at[j], out_ref.at[m], out_sems.at[j]))
            stores[-1].start()
    for copy in stores:
        copy.wait()


def added(parts_ref, out_ref):
    out_ref[...] = jnp.sum(parts_ref[:, 0], axis=0)


def finish(n, tile, scale, active_ref, mirrored, late, *refs):
    arrived, (precision_ref, out_ref) = refs[:-2], refs[-2:]
    z, y, k = (lax.axis_index(a) for a in AXES)
    row = lax.broadcasted_iota(jnp.int32, (tile, tile), 0)
    column = lax.broadcasted_iota(jnp.int32, (tile, tile), 1)

    def put(d, total):
        t = lax.rem(y + d, n)
        w = precision_ref[t]
        gradient = total * scale + RIDGE * w
        if d == 0:
            on_diag = (row == column) & (lax.rem(2 * k - z + n, n) == 0)
            inverse = jnp.where(on_diag, 1.0 / jnp.where(on_diag, w, 1.0), 0.0)
            stepped = w - STEP * (gradient - inverse)
        else:
            stepped = w - STEP * gradient
        shrunk = jnp.where(
            stepped > 0, jnp.maximum(stepped - STEP * LASSO, 0.0), jnp.minimum(stepped + STEP * LASSO, 0.0)
        )
        if d == 0:
            shrunk = jnp.where(on_diag, stepped, shrunk)
        out_ref[t] = shrunk * active_ref[t].astype(jnp.float32)

    put(LATE, late[...])
    for i, d in enumerate(EARLY):
        put(d, mirrored[i])
    for d, ref in zip((LATE,) + tuple(EARLY[i] for i in TURNED), arrived):
        put(n - d, ref[...].T)


def local(n, resid, samples, precision, active):
    tile, depth = resid.shape
    vmem, smem, far = (pl.BlockSpec(memory_space=s) for s in (pltpu.VMEM, pltpu.SMEM, pltpu.HBM))

    def moved(a, to):
        def index(z, y, k):
            return (z % n * n + y % n) * n + k % n

        ids = [(z, y, k) for z in range(n) for y in range(n) for k in range(n)]
        return lax.ppermute(a, AXES, [(index(*i), index(*to(*i))) for i in ids])

    own = pl.pallas_call(
        join,
        out_shape=jax.ShapeDtypeStruct((tile, 2 * depth), resid.dtype),
        in_specs=[vmem, vmem],
        out_specs=vmem,
        compiler_params=pltpu.CompilerParams(vmem_limit_bytes=60 * MIB),
    )(resid, samples)
    rows = lax.all_gather(own, "k", axis=0, tiled=True)
    panel = {d: moved(own, lambda z, y, k, d=d: (z, y - d, k)) for d in SENT}

    def multiplied(columns, offset, flops):
        count = len(columns) + offset
        return pl.pallas_call(
            functools.partial(products, n, tile, depth, count, offset),
            out_shape=jax.ShapeDtypeStruct((n, count, tile, tile), jnp.float32),
            in_specs=[far] + [vmem] * len(columns),
            out_specs=far,
            scratch_shapes=[
                pltpu.VMEM((CHUNKS, n // CHUNKS * tile, 2 * depth), jnp.bfloat16),
                pltpu.VMEM((count * tile, 2 * depth), jnp.bfloat16),
                pltpu.VMEM((n, count, tile, tile), jnp.float32),
                pltpu.SemaphoreType.DMA((2,)),
                pltpu.SemaphoreType.DMA((CHUNKS,)),
                pltpu.SemaphoreType.DMA((n,)),
            ],
            compiler_params=pltpu.CompilerParams(vmem_limit_bytes=52 * MIB),
            cost_estimate=pl.CostEstimate(flops=flops, bytes_accessed=6 * MIB, transcendentals=0),
        )(rows, *columns)

    once = 4 * n * tile * tile * depth
    early = lax.psum_scatter(
        multiplied([panel[d] for d in EARLY[1:]], 1, once), "z", scatter_dimension=0, tiled=True
    )[0]
    weight = 600 * once
    parts = lax.all_to_all(multiplied([panel[LATE]], 0, weight), "z", 0, 0, tiled=True)
    late = pl.pallas_call(
        added,
        out_shape=jax.ShapeDtypeStruct((tile, tile), jnp.float32),
        in_specs=[vmem],
        out_specs=vmem,
        compiler_params=pltpu.CompilerParams(vmem_limit_bytes=16 * MIB),
    )(parts)
    arrived = [moved(late, lambda z, y, k: (z, y + LATE, k))]
    late = moved(late, lambda z, y, k: (z, y, z - k))
    mirrored = moved(early, lambda z, y, k: (z, y, z - k))
    arrived += [moved(early[i], lambda z, y, k, d=EARLY[i]: (z, y + d, k)) for i in TURNED]
    updated = pl.pallas_call(
        functools.partial(finish, n, tile, 0.5 / (depth * n)),
        out_shape=jax.ShapeDtypeStruct((n, tile, tile), jnp.float32),
        in_specs=[smem] + [vmem] * (3 + len(arrived)),
        out_specs=vmem,
        compiler_params=pltpu.CompilerParams(vmem_limit_bytes=16 * MIB),
    )(active.reshape(n), mirrored, late, *arrived, precision.reshape(n, tile, tile))
    return updated.reshape(precision.shape)


def solution(mesh):
    n = mesh.shape["blk"]
    grid = Mesh(mesh.devices.reshape(n, n, n), AXES)
    rows = ("y", "k")
    in_specs = (P(rows, "z"), P(rows, "z"), P(rows, "z"), P(rows, "z"))
    return jax.shard_map(
        functools.partial(local, n), mesh=grid, in_specs=in_specs, out_specs=P(rows, "z"), check_vma=False
    )
```

```python
import functools

import jax
import jax.numpy as jnp
from jax import lax
from jax.experimental import pallas as pl
from jax.experimental.pallas import tpu as pltpu
from jax.sharding import Mesh, PartitionSpec as P

STEP = 1.0
LASSO = 0.1
RIDGE = 0.5
AXES = ("z", "y", "k")
EARLY = (0, 1, 6, 4)
TURNED = (1, 2)
LATE = 3
SENT = (1, 6, 3, 4)
CHUNKS = 2
MIB = 2**20


def join(a_ref, b_ref, out_ref):
    half = a_ref.shape[1]
    out_ref[:, :half] = a_ref[...]
    out_ref[:, half:] = b_ref[...]


def products(n, tile, depth, count, offset, rows_ref, *refs):
    columns, (out_ref, rows, picked, made, own_sems, row_sems, out_sems) = refs[:count - offset], refs[count - offset:]
    k = lax.axis_index("k")
    per = n // CHUNKS
    chunks = [
        pltpu.make_async_copy(rows_ref.at[pl.ds(c * per * tile, per * tile)], rows.at[c], row_sems.at[c])
        for c in range(CHUNKS)
    ]
    here = [
        pltpu.make_async_copy(
            rows_ref.at[pl.ds(pl.multiple_of(k * tile, tile), tile), pl.ds((1 - h) * depth, depth)],
            picked.at[pl.ds(0, tile), pl.ds(h * depth, depth)],
            own_sems.at[h],
        )
        for h in range(2 * offset)
    ]
    for copy in here + chunks:
        copy.start()
    for i, ref in enumerate(columns, offset):
        picked[i * tile:(i + 1) * tile, :depth] = ref[:, depth:]
        picked[i * tile:(i + 1) * tile, depth:] = ref[:, :depth]
    for copy in here:
        copy.wait()
    stores = []
    for c in range(CHUNKS):
        chunks[c].wait()
        part = lax.dot_general(
            rows[c], picked[...], (((1,), (1,)), ((), ())), preferred_element_type=jnp.float32
        )
        for e in range(per):
            j = c * per + e
            for i in range(count):
                made[j, i] = part[e * tile:(e + 1) * tile, i * tile:(i + 1) * tile]
            m = lax.rem(j + k, n)
            stores.append(pltpu.make_async_copy(made.at[j], out_ref.at[m], out_sems.at[j]))
            stores[-1].start()
    for copy in stores:
        copy.wait()


def added(parts_ref, out_ref):
    out_ref[...] = jnp.sum(parts_ref[:, 0], axis=0)


def finish(n, tile, scale, active_ref, mirrored, late, *refs):
    arrived, (precision_ref, out_ref) = refs[:-2], refs[-2:]
    z, y, k = (lax.axis_index(a) for a in AXES)
    row = lax.broadcasted_iota(jnp.int32, (tile, tile), 0)
    column = lax.broadcasted_iota(jnp.int32, (tile, tile), 1)

    def put(d, total):
        t = lax.rem(y + d, n)
        w = precision_ref[t]
        gradient = total * scale + RIDGE * w
        if d == 0:
            on_diag = (row == column) & (lax.rem(2 * k - z + n, n) == 0)
            inverse = jnp.where(on_diag, 1.0 / jnp.where(on_diag, w, 1.0), 0.0)
            stepped = w - STEP * (gradient - inverse)
        else:
            stepped = w - STEP * gradient
        shrunk = jnp.where(
            stepped > 0, jnp.maximum(stepped - STEP * LASSO, 0.0), jnp.minimum(stepped + STEP * LASSO, 0.0)
        )
        if d == 0:
            shrunk = jnp.where(on_diag, stepped, shrunk)
        out_ref[t] = shrunk * active_ref[t].astype(jnp.float32)

    put(LATE, late[...])
    for i, d in enumerate(EARLY):
        put(d, mirrored[i])
    for d, ref in zip((LATE,) + tuple(EARLY[i] for i in TURNED), arrived):
        put(n - d, ref[...].T)


def local(n, resid, samples, precision, active):
    tile, depth = resid.shape
    vmem, smem, far = (pl.BlockSpec(memory_space=s) for s in (pltpu.VMEM, pltpu.SMEM, pltpu.HBM))

    def moved(a, to):
        def index(z, y, k):
            return (z % n * n + y % n) * n + k % n

        ids = [(z, y, k) for z in range(n) for y in range(n) for k in range(n)]
        return lax.ppermute(a, AXES, [(index(*i), index(*to(*i))) for i in ids])

    own = pl.pallas_call(
        join,
        out_shape=jax.ShapeDtypeStruct((tile, 2 * depth), resid.dtype),
        in_specs=[vmem, vmem],
        out_specs=vmem,
        compiler_params=pltpu.CompilerParams(vmem_limit_bytes=60 * MIB),
    )(resid, samples)
    rows = lax.all_gather(own, "k", axis=0, tiled=True)
    panel = {d: moved(own, lambda z, y, k, d=d: (z, y - d, k)) for d in SENT}

    def multiplied(columns, offset, flops):
        count = len(columns) + offset
        return pl.pallas_call(
            functools.partial(products, n, tile, depth, count, offset),
            out_shape=jax.ShapeDtypeStruct((n, count, tile, tile), jnp.float32),
            in_specs=[far] + [vmem] * len(columns),
            out_specs=far,
            scratch_shapes=[
                pltpu.VMEM((CHUNKS, n // CHUNKS * tile, 2 * depth), jnp.bfloat16),
                pltpu.VMEM((count * tile, 2 * depth), jnp.bfloat16),
                pltpu.VMEM((n, count, tile, tile), jnp.float32),
                pltpu.SemaphoreType.DMA((2,)),
                pltpu.SemaphoreType.DMA((CHUNKS,)),
                pltpu.SemaphoreType.DMA((n,)),
            ],
            compiler_params=pltpu.CompilerParams(vmem_limit_bytes=52 * MIB),
            cost_estimate=pl.CostEstimate(flops=flops, bytes_accessed=6 * MIB, transcendentals=0),
        )(rows, *columns)

    once = 4 * n * tile * tile * depth
    early = lax.psum_scatter(
        multiplied([panel[d] for d in EARLY[1:]], 1, once), "z", scatter_dimension=0, tiled=True
    )[0]
    weight = 600 * once
    parts = lax.all_to_all(multiplied([panel[LATE]], 0, weight), "z", 0, 0, tiled=True)
    late = pl.pallas_call(
        added,
        out_shape=jax.ShapeDtypeStruct((tile, tile), jnp.float32),
        in_specs=[vmem],
        out_specs=vmem,
        compiler_params=pltpu.CompilerParams(vmem_limit_bytes=16 * MIB),
    )(parts)
    arrived = [moved(late, lambda z, y, k: (z, y + LATE, k))]
    late = moved(late, lambda z, y, k: (z, y, z - k))
    mirrored = moved(early, lambda z, y, k: (z, y, z - k))
    arrived += [moved(early[i], lambda z, y, k, d=EARLY[i]: (z, y + d, k)) for i in TURNED]
    updated = pl.pallas_call(
        functools.partial(finish, n, tile, 0.5 / (depth * n)),
        out_shape=jax.ShapeDtypeStruct((n, tile, tile), jnp.float32),
        in_specs=[smem] + [vmem] * (3 + len(arrived)),
        out_specs=vmem,
        compiler_params=pltpu.CompilerParams(vmem_limit_bytes=16 * MIB),
    )(active.reshape(n), mirrored, late, *arrived, precision.reshape(n, tile, tile))
    return updated.reshape(precision.shape)


def solution(mesh):
    n = mesh.shape["blk"]
    grid = Mesh(mesh.devices.reshape(n, n, n), AXES)
    rows = ("y", "k")
    in_specs = (P(rows, "z"), P(rows, "z"), P(rows, "z"), P(rows, "z"))
    return jax.shard_map(
        functools.partial(local, n), mesh=grid, in_specs=in_specs, out_specs=P(rows, "z"), check_vma=False
    )
```
